512 devices in a mesh: chan: 16 (over y, z_hi), tm: 32 (over x, z_lo, core).
Axes of the slice: x: 4, y: 8, z: 8 (z_hi: 2, z_lo: 4; z = z_hi * 4 + z_lo), core: 2. Of those that a mesh axis runs over, the one named last changes fastest.
Arguments:
- voltage: bfloat16 [24576, 2, 16, 1024], P('tm', None, 'chan'), may hold values from -8 to 8, as said below
- taps: float32 [256], replicated, may hold values from -0.375 to 0.375
Outputs:
- visibility: float32 [16, 2, 1024, 8192], P('chan', None, None, 'tm')
The draws below stay inside these ranges and needn't reach their ends.
Inputs may be any that keep to these rules, and one draw needn't show every extreme that they name: `voltage`: real and imaginary parts of sampled antenna voltages.
All inputs are finite; a program needn't handle non-finite values.
Results may differ from the reference program's by a relative error of at most 0.00068.
Values may be sent and summed in bfloat16 or wider, within the bound.
No kernel may reach another device: no remote copies, remote signals or barrier semaphores. Data moves between devices by JAX's collectives and lax.ppermute only.
A program may use at most 128 MiB of HBM per device.

```python
import jax
import jax.numpy as jnp
from jax import lax

S = 1024
FINE = 16
FOUT = 8
TAPS = 16
SAMPLES = 24576
FRAMES = 1536
CHANNELS = 16


def draw_voltage(key, part):
    key_common = jax.random.fold_in(key, 11)
    key_gain = jax.random.fold_in(key, 12)
    key_noise = jax.random.fold_in(key, 13)
    common = jax.random.normal(key_common, (SAMPLES, 2, CHANNELS, 1), jnp.float32)
    gains = jax.random.uniform(key_gain, (1, 1, 1, S), jnp.float32, 0.5, 1.5)
    noise = 0.7 * jax.random.normal(key_noise, (SAMPLES, 2, CHANNELS, S), jnp.float32)
    time_ramp = 0.6 * jnp.power(3.0, jnp.arange(SAMPLES, dtype=jnp.float32) / SAMPLES)
    values = time_ramp[:, None, None, None] * (common * gains + noise)
    return jnp.clip(values, -8.0, 8.0).astype(jnp.bfloat16)


def bell_draw(own_key, dims, deviation, bound, kind=jnp.bfloat16):
    return jnp.clip(deviation * jax.random.normal(own_key, dims, jnp.float32), -bound, bound).astype(kind)


def setup_inputs(seed: int = 0) -> dict:
    seeds = jax.random.split(jax.random.key(seed), 3)
    return {
        "voltage": draw_voltage(jax.random.fold_in(seeds[2], 71), 0),
        "taps": bell_draw(seeds[1], (TAPS * FINE,), (TAPS * FINE) ** -0.5, 0.375, jnp.float32),
    }


def coefficients(taps):
    fine_out = jnp.arange(FOUT, dtype=jnp.int32)
    fine_in = jnp.arange(FINE, dtype=jnp.int32)
    phase = ((fine_out[:, None] * fine_in[None, :]) % FINE).astype(jnp.float32) * (2.0 * jnp.pi / FINE)
    cosine = jnp.cos(phase)[:, :, None]
    sine_table = jnp.sin(phase)[:, :, None]
    tap_table = jnp.transpose(taps.reshape(TAPS, FINE))[None, :, :]
    real_row = jnp.stack([tap_table * cosine, tap_table * sine_table], 2)
    imag_row = jnp.stack([-tap_table * sine_table, tap_table * cosine], 2)
    coeff_table = jnp.stack([real_row, imag_row], 0)
    return coeff_table.reshape(2 * FOUT, FINE * 2, TAPS).astype(jnp.bfloat16)


def reference(voltage, taps):
    kernel = coefficients(taps).astype(jnp.float32)

    def one_channel(chan_idx):
        signal = lax.dynamic_index_in_dim(voltage, chan_idx, 2, keepdims=False)
        padded = jnp.pad(signal, (((TAPS - 1) * FINE, 0), (0, 0), (0, 0)))
        frame_input = padded.reshape(FRAMES + TAPS - 1, FINE * 2, S).astype(jnp.float32)
        filtered = lax.conv_general_dilated(frame_input, kernel, (1,), "VALID", dimension_numbers=("WCN", "OIW", "WCN"), precision=lax.Precision.HIGHEST)
        rounded = lax.optimization_barrier(filtered.astype(jnp.bfloat16))
        spectra = rounded.astype(jnp.float32).reshape(FRAMES, 2, FOUT, S)
        rotated = jnp.stack([spectra, jnp.stack([-spectra[:, 1], spectra[:, 0]], 1)], 0)

        def one_fine(fine_k):
            row_part = lax.dynamic_index_in_dim(rotated, fine_k, 3, keepdims=False)
            col_part = lax.dynamic_index_in_dim(spectra, fine_k, 2, keepdims=False)
            return jnp.einsum("pfrj,frs->pjs", row_part, col_part, precision=lax.Precision.HIGHEST) * (1.0 / FRAMES)

        blocks = lax.map(one_fine, jnp.arange(FOUT, dtype=jnp.int32))
        return jnp.transpose(blocks, (1, 2, 0, 3)).reshape(2, S, FOUT * S)

    return lax.map(one_channel, jnp.arange(CHANNELS, dtype=jnp.int32))
```

```python
import functools

import jax
import jax.numpy as jnp
import numpy as np
from jax import lax
from jax.experimental import pallas as pl
from jax.experimental.pallas import tpu as pltpu
from jax.sharding import PartitionSpec as P

FINE = 16
FOUT = 8
TAPS = 16
S = 1024
XS, ZS, CORES = 4, 4, 2
BLOCK = 16
ROWS = 2 * BLOCK
WINDOW = 2 * BLOCK * FINE
VMEM = pltpu.VMEM
F32 = jnp.float32
BF16 = jnp.bfloat16


def place(x, z, c):
    return (x * ZS + z) * CORES + c


def moves(rule):
    out = []
    for x in range(XS):
        for z in range(ZS):
            for c in range(CORES):
                out.append((place(x, z, c), place(*rule(x, z, c))))
    return out


def move(array, rule):
    return lax.ppermute(array, "tm", moves(rule))


def along_x(distance):
    return lambda x, z, c: ((x + distance) % XS, z, c)


def far_z(x, z, c):
    return x, z ^ 2, c


def near_z(x, z, c):
    return x, z ^ 1, c


def other_core(x, z, c):
    return x, z, 1 - c


def halo_of(tail):
    pairs = [(i, i + 1) for i in range(XS * ZS * CORES - 1)]
    return lax.ppermute(tail, "tm", pairs)


def trig_table():
    k = np.arange(FOUT)[:, None]
    n = np.arange(FINE)[None, :]
    phase = (k * n % FINE) * (2.0 * np.pi / FINE)
    c, s = np.cos(phase), np.sin(phase)
    real_row = np.stack([c, s], -1).reshape(FOUT, 2 * FINE)
    imag_row = np.stack([-s, c], -1).reshape(FOUT, 2 * FINE)
    rows = np.stack([real_row, imag_row], 1).reshape(2 * FOUT, 2 * FINE)
    return np.tile(rows.astype(np.float32), (1, 2 * BLOCK))


def spec(n):
    return [pl.BlockSpec(memory_space=VMEM)] * n


def shape(*dims, kind=BF16):
    return jax.ShapeDtypeStruct(dims, kind)


def band_matrix(taps_ref, trig_ref, band_ref):
    me = lax.axis_index("tm")
    x = me // (ZS * CORES)
    odd = me // 4 % 2
    width = 2 * WINDOW
    taps_len = TAPS * FINE
    row = lax.broadcasted_iota(jnp.int32, (taps_len, width), 0)
    col = lax.broadcasted_iota(jnp.int32, (taps_len, width), 1)
    pick = (col // 2 == row).astype(F32)
    taps = jnp.broadcast_to(taps_ref[...], (BLOCK, taps_len))
    twice = lax.dot_general(
        taps, pick, (((1,), (0,)), ((), ())), precision=lax.Precision.HIGHEST, preferred_element_type=F32
    )
    frame = lax.broadcasted_iota(jnp.int32, (BLOCK, width), 0)
    shifted = jnp.zeros((BLOCK, width), F32)
    for f in range(BLOCK):
        shifted = jnp.where(frame == f, pltpu.roll(twice, 2 * FINE * (f + 1) % width, 1), shifted)
    for d in range(XS):
        for other in range(2):
            k = (x + d) % XS * 2 + (odd + other) % 2
            for ro in range(2):
                at = ((d * 2 + other) * 2 + ro) * BLOCK
                wave = trig_ref[pl.ds(k * 2 + ro, 1), :]
                band_ref[at : at + BLOCK, :] = (shifted * wave).astype(BF16)


def filter_late(taps_ref, trig_ref, volt_ref, band_ref, m0, m1, m2, m3, t_ref):
    band_matrix(taps_ref, trig_ref, band_ref)
    mine = (m0, m1, m2, m3)
    for i in range(2):
        start = i * BLOCK * FINE
        window = volt_ref[start : start + WINDOW].reshape(2 * WINDOW, S)
        out = jnp.dot(band_ref[...], window, preferred_element_type=F32).astype(BF16)
        rows = slice(i * ROWS, (i + 1) * ROWS)
        for d in range(XS):
            mine[d][rows, :] = out[2 * d * ROWS : (2 * d + 1) * ROWS]
            t_ref[d, rows, :] = out[(2 * d + 1) * ROWS : (2 * d + 2) * ROWS]


def filter_first(halo_ref, volt_ref, band_ref, m_ref, t_ref):
    here = BLOCK * FINE
    own = volt_ref[0:here].reshape(2 * here, S)
    prior = halo_ref[...].reshape(2 * here - 2 * FINE, S)
    band = band_ref[...]
    out = jnp.dot(band[:, 2 * here :], own, preferred_element_type=F32)
    out += jnp.dot(band[:, 2 * FINE : 2 * here], prior, preferred_element_type=F32)
    out = out.astype(BF16)
    for d in range(XS):
        m_ref[d] = out[2 * d * ROWS : (2 * d + 1) * ROWS]
        t_ref[d] = out[(2 * d + 1) * ROWS : (2 * d + 2) * ROWS]


def products(n_pieces, scale, *refs):
    pieces, rest = refs[:n_pieces], refs[n_pieces:]
    out_ref = rest[-1]
    j = pl.program_id(0)
    quarter = lax.axis_index("tm") % 4
    cols = pl.ds(pl.multiple_of(quarter * 256, 256), 256)
    rows = pl.ds(pl.multiple_of(j * 256, 256), 256)
    total = None
    for piece in pieces:
        n = piece.shape[0]
        here = piece[:, cols]
        halves = here.reshape(n // ROWS, 2, BLOCK, 256)
        turned = jnp.stack([halves[:, 1], -halves[:, 0]], 1).reshape(n, 256)
        both = jnp.concatenate([here, turned], 1)
        part = lax.dot_general(
            piece[:, rows], both, (((0,), (0,)), ((), ())), preferred_element_type=F32
        )
        total = part if total is None else total + part
    real, imag = total[:, :256], total[:, 256:]
    if len(rest) > 1:
        real += rest[0][0]
        imag += rest[0][1]
    if scale is not None:
        real, imag = real * scale, imag * scale
    out_ref[0] = real
    out_ref[1] = imag


def correlate(pieces, acc, scale=None):
    frames = sum(p.shape[0] for p in pieces)
    block = pl.BlockSpec((2, 256, 256), lambda j: (0, j, 0))
    more = [] if acc is None else [acc]
    return pl.pallas_call(
        functools.partial(products, len(pieces), scale),
        grid=(4,),
        out_shape=shape(2, S, 256, kind=F32),
        in_specs=[pl.BlockSpec(p.shape, lambda j: (0, 0), memory_space=VMEM, pipeline_mode=pl.Buffered(1)) for p in pieces]
        + [block] * len(more),
        out_specs=block,
        compiler_params=pltpu.CompilerParams(vmem_limit_bytes=40 << 20),
        cost_estimate=pl.CostEstimate(flops=2 * frames * S * 512, bytes_accessed=4 << 20, transcendentals=0),
    )(*pieces, *more)


def shards(voltage, taps):
    samples_here = voltage.shape[0]
    late = 2 * BLOCK
    volt = voltage.reshape(samples_here, 2, S)
    halo = halo_of(volt[samples_here - (TAPS - 1) * FINE :])
    params = pltpu.CompilerParams(vmem_limit_bytes=40 << 20)
    band, ma0, ma1, ma2, ma3, ta = pl.pallas_call(
        filter_late,
        out_shape=(
            shape(4 * FOUT * BLOCK // 2, 2 * WINDOW),
            *[shape(2 * late, S)] * 4,
            shape(XS, 2 * late, S),
        ),
        in_specs=spec(3),
        out_specs=spec(6),
        compiler_params=params,
        cost_estimate=pl.CostEstimate(flops=2 << 29, bytes_accessed=6 << 20, transcendentals=0),
    )(taps.reshape(1, -1), jnp.asarray(trig_table()), volt)
    ta = move(ta, far_z)
    ma = [ma0] + [move(m, along_x(d)) for d, m in ((1, ma1), (2, ma2), (3, ma3))]
    mb, tb = pl.pallas_call(
        filter_first,
        out_shape=(shape(XS, ROWS, S), shape(XS, ROWS, S)),
        in_specs=spec(3),
        out_specs=spec(2),
        compiler_params=params,
        cost_estimate=pl.CostEstimate(flops=1 << 29, bytes_accessed=3 << 20, transcendentals=0),
    )(halo, volt, band)
    tb = move(tb, far_z)
    ma = jnp.concatenate(ma, 0)
    ma = jnp.concatenate([ma, move(ma, near_z)], 0)
    second = [jnp.concatenate([ta[d], mb[d]], 0) for d in range(XS)]
    second = [second[0]] + [move(second[d], along_x(d)) for d in range(1, XS)]
    second = jnp.concatenate(second, 0)
    third = [tb[0]] + [move(tb[d], along_x(d)) for d in range(1, XS)]
    third = jnp.concatenate(third, 0)
    second = jnp.concatenate([second, move(second, near_z)], 0)
    third_near = move(third, near_z)
    acc = correlate([ma, move(ma, other_core)], None)
    acc = correlate([second, move(second, other_core)], acc)
    pieces = [third, move(third, other_core), third_near, move(third_near, other_core)]
    frames = samples_here // FINE * XS * ZS * CORES
    return correlate(pieces, acc, 1.0 / frames)[None]


def solution(mesh):
    in_specs = (P("tm", None, "chan", None), P())
    out_specs = P("chan", None, None, "tm")
    return jax.shard_map(shards, mesh=mesh, in_specs=in_specs, out_specs=out_specs, check_vma=False)
```

```python
import functools

import jax
import jax.numpy as jnp
import numpy as np
from jax import lax
from jax.experimental import pallas as pl
from jax.experimental.pallas import tpu as pltpu
from jax.sharding import PartitionSpec as P

FINE = 16
FOUT = 8
TAPS = 16
S = 1024
XS, ZS, CORES = 4, 4, 2
BLOCK = 16
ROWS = 2 * BLOCK
WINDOW = 2 * BLOCK * FINE
VMEM = pltpu.VMEM
F32 = jnp.float32
BF16 = jnp.bfloat16


def place(x, z, c):
    return (x * ZS + z) * CORES + c


def moves(rule):
    out = []
    for x in range(XS):
        for z in range(ZS):
            for c in range(CORES):
                out.append((place(x, z, c), place(*rule(x, z, c))))
    return out


def move(array, rule):
    return lax.ppermute(array, "tm", moves(rule))


def along_x(distance):
    return lambda x, z, c: ((x + distance) % XS, z, c)


def far_z(x, z, c):
    return x, z ^ 2, c


def near_z(x, z, c):
    return x, z ^ 1, c


def other_core(x, z, c):
    return x, z, 1 - c


def halo_of(tail):
    pairs = [(i, i + 1) for i in range(XS * ZS * CORES - 1)]
    return lax.ppermute(tail, "tm", pairs)


def trig_table():
    k = np.arange(FOUT)[:, None]
    n = np.arange(FINE)[None, :]
    phase = (k * n % FINE) * (2.0 * np.pi / FINE)
    c, s = np.cos(phase), np.sin(phase)
    real_row = np.stack([c, s], -1).reshape(FOUT, 2 * FINE)
    imag_row = np.stack([-s, c], -1).reshape(FOUT, 2 * FINE)
    rows = np.stack([real_row, imag_row], 1).reshape(2 * FOUT, 2 * FINE)
    return np.tile(rows.astype(np.float32), (1, 2 * BLOCK))


def spec(n):
    return [pl.BlockSpec(memory_space=VMEM)] * n


def shape(*dims, kind=BF16):
    return jax.ShapeDtypeStruct(dims, kind)


def band_matrix(taps_ref, trig_ref, band_ref):
    me = lax.axis_index("tm")
    x = me // (ZS * CORES)
    odd = me // 4 % 2
    width = 2 * WINDOW
    taps_len = TAPS * FINE
    row = lax.broadcasted_iota(jnp.int32, (taps_len, width), 0)
    col = lax.broadcasted_iota(jnp.int32, (taps_len, width), 1)
    pick = (col // 2 == row).astype(F32)
    taps = jnp.broadcast_to(taps_ref[...], (BLOCK, taps_len))
    twice = lax.dot_general(
        taps, pick, (((1,), (0,)), ((), ())), precision=lax.Precision.HIGHEST, preferred_element_type=F32
    )
    frame = lax.broadcasted_iota(jnp.int32, (BLOCK, width), 0)
    shifted = jnp.zeros((BLOCK, width), F32)
    for f in range(BLOCK):
        shifted = jnp.where(frame == f, pltpu.roll(twice, 2 * FINE * (f + 1) % width, 1), shifted)
    for d in range(XS):
        for other in range(2):
            k = (x + d) % XS * 2 + (odd + other) % 2
            for ro in range(2):
                at = ((d * 2 + other) * 2 + ro) * BLOCK
                wave = trig_ref[pl.ds(k * 2 + ro, 1), :]
                band_ref[at : at + BLOCK, :] = (shifted * wave).astype(BF16)


def filter_late(taps_ref, trig_ref, volt_ref, band_ref, *out_refs):
    band_matrix(taps_ref, trig_ref, band_ref)
    for i in range(2):
        start = i * BLOCK * FINE
        window = volt_ref[start : start + WINDOW].reshape(2 * WINDOW, S)
        out = jnp.dot(band_ref[...], window, preferred_element_type=F32).astype(BF16)
        for d in range(XS):
            for other in range(2):
                at = (2 * other + i) * ROWS
                out_refs[d][at : at + ROWS, :] = out[(2 * d + other) * ROWS : (2 * d + other + 1) * ROWS]


def filter_first(halo_ref, volt_ref, band_ref, *out_refs):
    here = BLOCK * FINE
    own = volt_ref[0:here].reshape(2 * here, S)
    prior = halo_ref[...].reshape(2 * here - 2 * FINE, S)
    band = band_ref[...]
    out = jnp.dot(band[:, 2 * here :], own, preferred_element_type=F32)
    out += jnp.dot(band[:, 2 * FINE : 2 * here], prior, preferred_element_type=F32)
    out = out.astype(BF16)
    for d in range(XS):
        out_refs[d][...] = out[2 * d * ROWS : 2 * (d + 1) * ROWS]


def products(n_pieces, scale, *refs):
    pieces, rest = refs[:n_pieces], refs[n_pieces:]
    out_ref = rest[-1]
    j = pl.program_id(0)
    quarter = lax.axis_index("tm") % 4
    cols = pl.ds(pl.multiple_of(quarter * 256, 256), 256)
    rows = pl.ds(pl.multiple_of(j * 256, 256), 256)
    total = None
    for piece in pieces:
        n = piece.shape[0]
        here = piece[:, cols]
        halves = here.reshape(n // ROWS, 2, BLOCK, 256)
        turned = jnp.stack([halves[:, 1], -halves[:, 0]], 1).reshape(n, 256)
        both = jnp.concatenate([here, turned], 1)
        part = lax.dot_general(
            piece[:, rows], both, (((0,), (0,)), ((), ())), preferred_element_type=F32
        )
        total = part if total is None else total + part
    real, imag = total[:, :256], total[:, 256:]
    if len(rest) > 1:
        real += rest[0][0]
        imag += rest[0][1]
    if scale is not None:
        real, imag = real * scale, imag * scale
    out_ref[0] = real
    out_ref[1] = imag


def correlate(pieces, acc, scale=None):
    frames = sum(p.shape[0] for p in pieces)
    block = pl.BlockSpec((2, 256, 256), lambda j: (0, j, 0))
    more = [] if acc is None else [acc]
    return pl.pallas_call(
        functools.partial(products, len(pieces), scale),
        grid=(4,),
        out_shape=shape(2, S, 256, kind=F32),
        in_specs=[pl.BlockSpec(p.shape, lambda j: (0, 0), memory_space=VMEM, pipeline_mode=pl.Buffered(1)) for p in pieces]
        + [block] * len(more),
        out_specs=block,
        compiler_params=pltpu.CompilerParams(vmem_limit_bytes=40 << 20),
        cost_estimate=pl.CostEstimate(flops=2 * frames * S * 512, bytes_accessed=4 << 20, transcendentals=0),
    )(*pieces, *more)


def spread(slabs):
    return [slabs[0]] + [move(slabs[d], along_x(d)) for d in range(1, XS)]


def part(slabs, other):
    half = slabs[0].shape[0] // 2
    return jnp.concatenate([slab[other * half : (other + 1) * half] for slab in slabs], 0)


def shards(voltage, taps):
    samples_here = voltage.shape[0]
    volt = voltage.reshape(samples_here, 2, S)
    halo = halo_of(volt[samples_here - (TAPS - 1) * FINE :])
    params = pltpu.CompilerParams(vmem_limit_bytes=40 << 20)
    band, *late_out = pl.pallas_call(
        filter_late,
        out_shape=(shape(4 * FOUT * BLOCK // 2, 2 * WINDOW), *[shape(4 * ROWS, S)] * XS),
        in_specs=spec(3),
        out_specs=spec(1 + XS),
        compiler_params=params,
        cost_estimate=pl.CostEstimate(flops=2 << 29, bytes_accessed=6 << 20, transcendentals=0),
    )(taps.reshape(1, -1), jnp.asarray(trig_table()), volt)
    late_all = spread(late_out)
    halo, *late_all = lax.optimization_barrier((halo, *late_all))
    first_out = pl.pallas_call(
        filter_first,
        out_shape=[shape(2 * ROWS, S)] * XS,
        in_specs=spec(3),
        out_specs=spec(XS),
        compiler_params=params,
        cost_estimate=pl.CostEstimate(flops=1 << 29, bytes_accessed=3 << 20, transcendentals=0),
    )(halo, volt, band)
    ta = move(part(late_all, 1), far_z)
    ma = part(late_all, 0)
    ma_near = move(ma, near_z)
    first_all = spread(first_out)
    ta, ma_near, *first_all = lax.optimization_barrier((ta, ma_near, *first_all))
    tb = move(part(first_all, 1), far_z)
    second = jnp.concatenate([ta, part(first_all, 0)], 0)
    second_near = move(second, near_z)
    tb_near = move(tb, near_z)
    ma = jnp.concatenate([ma, ma_near], 0)
    acc = correlate([ma, move(ma, other_core)], None)
    own = jnp.concatenate([second, tb], 0)
    acc = correlate([own, move(own, other_core)], acc)
    near = jnp.concatenate(lax.optimization_barrier((second_near, tb_near)), 0)
    pieces = [near, move(near, other_core)]
    frames = samples_here // FINE * XS * ZS * CORES
    return correlate(pieces, acc, 1.0 / frames)[None]


def solution(mesh):
    in_specs = (P("tm", None, "chan", None), P())
    out_specs = P("chan", None, None, "tm")
    return jax.shard_map(shards, mesh=mesh, in_specs=in_specs, out_specs=out_specs, check_vma=False)
```

```python
import functools

import jax
import jax.numpy as jnp
import numpy as np
from jax import lax
from jax.experimental import pallas as pl
from jax.experimental.pallas import tpu as pltpu
from jax.sharding import PartitionSpec as P

FINE = 16
FOUT = 8
TAPS = 16
S = 1024
XS, ZS, CORES = 4, 4, 2
BLOCK = 16
ROWS = 2 * BLOCK
WINDOW = 2 * BLOCK * FINE
VMEM = pltpu.VMEM
F32 = jnp.float32
BF16 = jnp.bfloat16


def place(x, z, c):
    return (x * ZS + z) * CORES + c


def moves(rule):
    out = []
    for x in range(XS):
        for z in range(ZS):
            for c in range(CORES):
                out.append((place(x, z, c), place(*rule(x, z, c))))
    return out


def move(array, rule):
    return lax.ppermute(array, "tm", moves(rule))


def along_x(distance):
    return lambda x, z, c: ((x + distance) % XS, z, c)


def far_z(x, z, c):
    return x, z ^ 2, c


def near_z(x, z, c):
    return x, z ^ 1, c


def other_core(x, z, c):
    return x, z, 1 - c


def halo_of(tail):
    pairs = [(i, i + 1) for i in range(XS * ZS * CORES - 1)]
    return lax.ppermute(tail, "tm", pairs)


def trig_table():
    k = np.arange(FOUT)[:, None]
    n = np.arange(FINE)[None, :]
    phase = (k * n % FINE) * (2.0 * np.pi / FINE)
    c, s = np.cos(phase), np.sin(phase)
    real_row = np.stack([c, s], -1).reshape(FOUT, 2 * FINE)
    imag_row = np.stack([-s, c], -1).reshape(FOUT, 2 * FINE)
    rows = np.stack([real_row, imag_row], 1).reshape(2 * FOUT, 2 * FINE)
    return np.tile(rows.astype(np.float32), (1, 2 * BLOCK))


def spec(n):
    return [pl.BlockSpec(memory_space=VMEM)] * n


def shape(*dims, kind=BF16):
    return jax.ShapeDtypeStruct(dims, kind)


def band_matrix(taps_ref, trig_ref, band_ref):
    me = lax.axis_index("tm")
    x = me // (ZS * CORES)
    odd = me // 4 % 2
    width = 2 * WINDOW
    taps_len = TAPS * FINE
    row = lax.broadcasted_iota(jnp.int32, (taps_len, width), 0)
    col = lax.broadcasted_iota(jnp.int32, (taps_len, width), 1)
    pick = (col // 2 == row).astype(F32)
    taps = jnp.broadcast_to(taps_ref[...], (BLOCK, taps_len))
    twice = lax.dot_general(
        taps, pick, (((1,), (0,)), ((), ())), precision=lax.Precision.HIGHEST, preferred_element_type=F32
    )
    frame = lax.broadcasted_iota(jnp.int32, (BLOCK, width), 0)
    shifted = jnp.zeros((BLOCK, width), F32)
    for f in range(BLOCK):
        shifted = jnp.where(frame == f, pltpu.roll(twice, 2 * FINE * (f + 1) % width, 1), shifted)
    for d in range(XS):
        for other in range(2):
            k = (x + d) % XS * 2 + (odd + other) % 2
            for ro in range(2):
                at = ((d * 2 + other) * 2 + ro) * BLOCK
                wave = trig_ref[pl.ds(k * 2 + ro, 1), :]
                band_ref[at : at + BLOCK, :] = (shifted * wave).astype(BF16)


def filter_late(taps_ref, trig_ref, volt_ref, m0, m1, m2, m3, t_ref, band_ref):
    band_matrix(taps_ref, trig_ref, band_ref)
    for i in range(2):
        start = i * BLOCK * FINE
        window = volt_ref[start : start + WINDOW].reshape(2 * WINDOW, S)
        out = jnp.dot(band_ref[...], window, preferred_element_type=F32).astype(BF16)
        rows = slice(i * ROWS, (i + 1) * ROWS)
        for d, m_ref in enumerate((m0, m1, m2, m3)):
            m_ref[rows, :] = out[2 * d * ROWS : (2 * d + 1) * ROWS]
            t_ref[d, rows, :] = out[(2 * d + 1) * ROWS : (2 * d + 2) * ROWS]


def filter_first(halo_ref, volt_ref, band_ref, m_ref, t_ref):
    here = BLOCK * FINE
    own = volt_ref[0:here].reshape(2 * here, S)
    prior = halo_ref[...].reshape(2 * here - 2 * FINE, S)
    band = band_ref[...]
    out = jnp.dot(band[:, 2 * here :], own, preferred_element_type=F32)
    out += jnp.dot(band[:, 2 * FINE : 2 * here], prior, preferred_element_type=F32)
    out = out.astype(BF16)
    for d in range(XS):
        m_ref[d] = out[2 * d * ROWS : (2 * d + 1) * ROWS]
        t_ref[d] = out[(2 * d + 1) * ROWS : (2 * d + 2) * ROWS]


def products(n_pieces, scale, *refs):
    pieces, rest = refs[:n_pieces], refs[n_pieces:]
    out_ref = rest[-1]
    j = pl.program_id(0)
    quarter = lax.axis_index("tm") % 4
    cols = pl.ds(pl.multiple_of(quarter * 256, 256), 256)
    rows = pl.ds(pl.multiple_of(j * 256, 256), 256)
    total = None
    for piece in pieces:
        n = piece.shape[0]
        here = piece[:, cols]
        halves = here.reshape(n // ROWS, 2, BLOCK, 256)
        turned = jnp.stack([halves[:, 1], -halves[:, 0]], 1).reshape(n, 256)
        both = jnp.concatenate([here, turned], 1)
        part = lax.dot_general(
            piece[:, rows], both, (((0,), (0,)), ((), ())), preferred_element_type=F32
        )
        total = part if total is None else total + part
    real, imag = total[:, :256], total[:, 256:]
    if len(rest) > 1:
        real += rest[0][0]
        imag += rest[0][1]
    if scale is not None:
        real, imag = real * scale, imag * scale
    out_ref[0] = real
    out_ref[1] = imag


def correlate(pieces, acc, scale=None):
    frames = sum(p.shape[0] for p in pieces)
    block = pl.BlockSpec((2, 256, 256), lambda j: (0, j, 0))
    more = [] if acc is None else [acc]
    return pl.pallas_call(
        functools.partial(products, len(pieces), scale),
        grid=(4,),
        out_shape=shape(2, S, 256, kind=F32),
        in_specs=[pl.BlockSpec(p.shape, lambda j: (0, 0), memory_space=VMEM, pipeline_mode=pl.Buffered(1)) for p in pieces]
        + [block] * len(more),
        out_specs=block,
        compiler_params=pltpu.CompilerParams(vmem_limit_bytes=40 << 20),
        cost_estimate=pl.CostEstimate(flops=16 * frames * S * 512, bytes_accessed=4 << 20, transcendentals=0),
    )(*pieces, *more)


def spread(slabs):
    return [slabs[0]] + [move(slabs[d], along_x(d)) for d in range(1, XS)]


def shards(voltage, taps):
    samples_here = voltage.shape[0]
    volt = voltage.reshape(samples_here, 2, S)
    halo = halo_of(volt[samples_here - (TAPS - 1) * FINE :])
    params = pltpu.CompilerParams(vmem_limit_bytes=40 << 20)
    *late_out, band = pl.pallas_call(
        filter_late,
        out_shape=(*[shape(2 * ROWS, S)] * XS, shape(XS, 2 * ROWS, S), shape(16 * BLOCK, 2 * WINDOW)),
        in_specs=spec(3),
        out_specs=spec(XS + 2),
        compiler_params=params,
        cost_estimate=pl.CostEstimate(flops=2 << 29, bytes_accessed=6 << 20, transcendentals=0),
    )(taps.reshape(1, -1), jnp.asarray(trig_table()), volt)
    ma = spread(late_out[:XS])
    halo, *ma = lax.optimization_barrier((halo, *ma))
    ma = jnp.concatenate(ma, 0)
    ma_near = move(ma, near_z)
    ta = move(late_out[XS], far_z)
    first_out = pl.pallas_call(
        filter_first,
        out_shape=[shape(XS, ROWS, S)] * 2,
        in_specs=spec(3),
        out_specs=spec(2),
        compiler_params=params,
        cost_estimate=pl.CostEstimate(flops=1 << 29, bytes_accessed=3 << 20, transcendentals=0),
    )(halo, volt, band)
    mb, tb = first_out
    mb_near = move(mb, near_z)
    tb = move(tb, far_z)
    ta, ma_near = lax.optimization_barrier((ta, ma_near))
    second = spread([jnp.concatenate([ta[d], mb[d]], 0) for d in range(XS)])
    tb, mb_near, *second = lax.optimization_barrier((tb, mb_near, *second))
    ta = jnp.concatenate([slab[: 2 * ROWS] for slab in second], 0)
    ta_near = move(ta, near_z)
    third = spread([jnp.concatenate([tb[d], mb_near[d]], 0) for d in range(XS)])
    tb_near = move(jnp.concatenate([slab[:ROWS] for slab in third], 0), near_z)
    second, third = jnp.concatenate(second, 0), jnp.concatenate(third, 0)
    ma = jnp.concatenate([ma, ma_near], 0)
    acc = correlate([ma, move(ma, other_core), second, move(second, other_core), ta_near], None)
    acc, ta_near, tb_near = lax.optimization_barrier((acc, ta_near, tb_near))
    near = move(jnp.concatenate([ta_near, tb_near], 0), other_core)
    pieces = [third, move(third, other_core), tb_near, near]
    frames = samples_here // FINE * XS * ZS * CORES
    return correlate(pieces, acc, 1.0 / frames)[None]


def solution(mesh):
    in_specs = (P("tm", None, "chan", None), P())
    out_specs = P("chan", None, None, "tm")
    return jax.shard_map(shards, mesh=mesh, in_specs=in_specs, out_specs=out_specs, check_vma=False)
```

```python
import functools

import jax
import jax.numpy as jnp
import numpy as np
from jax import lax
from jax.experimental import pallas as pl
from jax.experimental.pallas import tpu as pltpu
from jax.sharding import PartitionSpec as P

FINE = 16
FOUT = 8
TAPS = 16
S = 1024
XS, ZS, CORES = 4, 4, 2
BLOCK = 16
ROWS = 2 * BLOCK
WINDOW = 2 * BLOCK * FINE
VMEM = pltpu.VMEM
F32 = jnp.float32
BF16 = jnp.bfloat16


def place(x, z, c):
    return (x * ZS + z) * CORES + c


def moves(rule):
    out = []
    for x in range(XS):
        for z in range(ZS):
            for c in range(CORES):
                out.append((place(x, z, c), place(*rule(x, z, c))))
    return out


def move(array, rule):
    return lax.ppermute(array, "tm", moves(rule))


def along_x(distance):
    return lambda x, z, c: ((x + distance) % XS, z, c)


def far_z(x, z, c):
    return x, z ^ 2, c


def near_z(x, z, c):
    return x, z ^ 1, c


def other_core(x, z, c):
    return x, z, 1 - c


def halo_of(tail):
    pairs = [(i, i + 1) for i in range(XS * ZS * CORES - 1)]
    return lax.ppermute(tail, "tm", pairs)


def trig_table():
    k = np.arange(FOUT)[:, None]
    n = np.arange(FINE)[None, :]
    phase = (k * n % FINE) * (2.0 * np.pi / FINE)
    c, s = np.cos(phase), np.sin(phase)
    real_row = np.stack([c, s], -1).reshape(FOUT, 2 * FINE)
    imag_row = np.stack([-s, c], -1).reshape(FOUT, 2 * FINE)
    rows = np.stack([real_row, imag_row], 1).reshape(2 * FOUT, 2 * FINE)
    return np.tile(rows.astype(np.float32), (1, 2 * BLOCK))


def spec(n):
    return [pl.BlockSpec(memory_space=VMEM)] * n


def shape(*dims, kind=BF16):
    return jax.ShapeDtypeStruct(dims, kind)


def band_matrix(taps_ref, trig_ref, band_ref):
    me = lax.axis_index("tm")
    x = me // (ZS * CORES)
    odd = me // 4 % 2
    width = 2 * WINDOW
    taps_len = TAPS * FINE
    row = lax.broadcasted_iota(jnp.int32, (taps_len, width), 0)
    col = lax.broadcasted_iota(jnp.int32, (taps_len, width), 1)
    pick = (col // 2 == row).astype(F32)
    taps = jnp.broadcast_to(taps_ref[...], (BLOCK, taps_len))
    twice = lax.dot_general(
        taps, pick, (((1,), (0,)), ((), ())), precision=lax.Precision.HIGHEST, preferred_element_type=F32
    )
    frame = lax.broadcasted_iota(jnp.int32, (BLOCK, width), 0)
    shifted = jnp.zeros((BLOCK, width), F32)
    for f in range(BLOCK):
        shifted = jnp.where(frame == f, pltpu.roll(twice, 2 * FINE * (f + 1) % width, 1), shifted)
    for d in range(XS):
        for other in range(2):
            k = (x + d) % XS * 2 + (odd + other) % 2
            for ro in range(2):
                at = ((d * 2 + other) * 2 + ro) * BLOCK
                wave = trig_ref[pl.ds(k * 2 + ro, 1), :]
                band_ref[at : at + BLOCK, :] = (shifted * wave).astype(BF16)


def tail_copy(volt_ref, out_ref, sem):
    n = out_ref.shape[0]
    copy = pltpu.make_async_copy(volt_ref.at[pl.ds(volt_ref.shape[0] - n, n)], out_ref, sem)
    copy.start()
    copy.wait()


def filter_late(taps_ref, trig_ref, volt_ref, m0, m1, m2, m3, t_ref, band_ref):
    band_matrix(taps_ref, trig_ref, band_ref)
    for i in range(2):
        start = i * BLOCK * FINE
        window = volt_ref[start : start + WINDOW].reshape(2 * WINDOW, S)
        out = jnp.dot(band_ref[...], window, preferred_element_type=F32).astype(BF16)
        rows = slice(i * ROWS, (i + 1) * ROWS)
        for d, m_ref in enumerate((m0, m1, m2, m3)):
            m_ref[rows, :] = out[2 * d * ROWS : (2 * d + 1) * ROWS]
            t_ref[d, rows, :] = out[(2 * d + 1) * ROWS : (2 * d + 2) * ROWS]


def filter_first(halo_ref, volt_ref, band_ref, m_ref, t_ref):
    here = BLOCK * FINE
    own = volt_ref[0:here].reshape(2 * here, S)
    prior = halo_ref[...].reshape(2 * here - 2 * FINE, S)
    band = band_ref[...]
    out = jnp.dot(band[:, 2 * here :], own, preferred_element_type=F32)
    out += jnp.dot(band[:, 2 * FINE : 2 * here], prior, preferred_element_type=F32)
    out = out.astype(BF16)
    for d in range(XS):
        m_ref[d] = out[2 * d * ROWS : (2 * d + 1) * ROWS]
        t_ref[d] = out[(2 * d + 1) * ROWS : (2 * d + 2) * ROWS]


def products(n_pieces, scale, *refs):
    pieces, rest = refs[:n_pieces], refs[n_pieces:]
    out_ref = rest[-1]
    j = pl.program_id(0)
    quarter = lax.axis_index("tm") % 4
    cols = pl.ds(pl.multiple_of(quarter * 256, 256), 256)
    rows = pl.ds(pl.multiple_of(j * 256, 256), 256)
    total = None
    for piece in pieces:
        n = piece.shape[0]
        here = piece[:, cols]
        halves = here.reshape(n // ROWS, 2, BLOCK, 256)
        turned = jnp.stack([halves[:, 1], -halves[:, 0]], 1).reshape(n, 256)
        both = jnp.concatenate([here, turned], 1)
        part = lax.dot_general(
            piece[:, rows], both, (((0,), (0,)), ((), ())), preferred_element_type=F32
        )
        total = part if total is None else total + part
    real, imag = total[:, :256], total[:, 256:]
    if len(rest) > 1:
        real += rest[0][0]
        imag += rest[0][1]
    if scale is not None:
        real, imag = real * scale, imag * scale
    out_ref[0] = real
    out_ref[1] = imag


def correlate(pieces, acc, scale=None):
    frames = sum(p.shape[0] for p in pieces)
    block = pl.BlockSpec((2, 256, 256), lambda j: (0, j, 0))
    more = [] if acc is None else [acc]
    return pl.pallas_call(
        functools.partial(products, len(pieces), scale),
        grid=(4,),
        out_shape=shape(2, S, 256, kind=F32),
        in_specs=[pl.BlockSpec(p.shape, lambda j: (0, 0), memory_space=VMEM, pipeline_mode=pl.Buffered(1)) for p in pieces]
        + [block] * len(more),
        out_specs=block,
        compiler_params=pltpu.CompilerParams(vmem_limit_bytes=40 << 20),
        cost_estimate=pl.CostEstimate(flops=16 * frames * S * 512, bytes_accessed=4 << 20, transcendentals=0),
    )(*pieces, *more)


def spread(slabs):
    return [slabs[0]] + [move(slabs[d], along_x(d)) for d in range(1, XS)]


def shards(voltage, taps):
    samples_here = voltage.shape[0]
    volt = voltage.reshape(samples_here, 2, S)
    params = pltpu.CompilerParams(vmem_limit_bytes=40 << 20)
    tail = pl.pallas_call(
        tail_copy,
        out_shape=shape((TAPS - 1) * FINE, 2, S),
        in_specs=[pl.BlockSpec(memory_space=VMEM)],
        out_specs=pl.BlockSpec(memory_space=VMEM),
        scratch_shapes=[pltpu.SemaphoreType.DMA],
        compiler_params=params,
    )(volt)
    halo = halo_of(tail)
    *late_out, band = pl.pallas_call(
        filter_late,
        out_shape=(*[shape(2 * ROWS, S)] * XS, shape(XS, 2 * ROWS, S), shape(16 * BLOCK, 2 * WINDOW)),
        in_specs=spec(3),
        out_specs=spec(XS + 2),
        compiler_params=params,
        cost_estimate=pl.CostEstimate(flops=2 << 29, bytes_accessed=6 << 20, transcendentals=0),
    )(taps.reshape(1, -1), jnp.asarray(trig_table()), volt)
    ma = spread(late_out[:XS])
    halo, *ma = lax.optimization_barrier((halo, *ma))
    ma = jnp.concatenate(ma, 0)
    ma_near, ma_near2 = move(ma[:ROWS], near_z), move(ma[ROWS:], near_z)
    ta = move(late_out[XS], far_z)
    first_out = pl.pallas_call(
        filter_first,
        out_shape=[shape(XS, ROWS, S)] * 2,
        in_specs=spec(3),
        out_specs=spec(2),
        compiler_params=params,
        cost_estimate=pl.CostEstimate(flops=1 << 29, bytes_accessed=3 << 20, transcendentals=0),
    )(halo, volt, band)
    mb, tb = first_out
    mb_near = move(mb, near_z)
    tb = move(tb, far_z)
    ta, ma_near = lax.optimization_barrier((ta, ma_near))
    second = spread([jnp.concatenate([ta[d], mb[d]], 0) for d in range(XS)])
    tb, mb_near, ma_near2, *second = lax.optimization_barrier((tb, mb_near, ma_near2, *second))
    ta = jnp.concatenate([slab[: 2 * ROWS] for slab in second], 0)
    ta_near = move(ta, near_z)
    third = spread([jnp.concatenate([tb[d], mb_near[d]], 0) for d in range(XS)])
    tb_near = move(jnp.concatenate([slab[:ROWS] for slab in third], 0), near_z)
    second, third = jnp.concatenate(second, 0), jnp.concatenate(third, 0)
    ma = jnp.concatenate([ma, ma_near, ma_near2, second], 0)
    acc = correlate([ma, move(ma, other_core), ta_near], None)
    acc, ta_near, tb_near = lax.optimization_barrier((acc, ta_near, tb_near))
    last = jnp.concatenate([tb_near, third], 0)
    pieces = [last, move(jnp.concatenate([last, ta_near], 0), other_core)]
    frames = samples_here // FINE * XS * ZS * CORES
    return correlate(pieces, acc, 1.0 / frames)[None]


def solution(mesh):
    in_specs = (P("tm", None, "chan", None), P())
    out_specs = P("chan", None, None, "tm")
    return jax.shard_map(shards, mesh=mesh, in_specs=in_specs, out_specs=out_specs, check_vma=False)
```

```python
import functools

import jax
import jax.numpy as jnp
import numpy as np
from jax import lax
from jax.experimental import pallas as pl
from jax.experimental.pallas import tpu as pltpu
from jax.sharding import PartitionSpec as P

FINE = 16
FOUT = 8
TAPS = 16
S = 1024
XS, ZS, CORES = 4, 4, 2
BLOCK = 16
ROWS = 2 * BLOCK
WINDOW = 2 * BLOCK * FINE
VMEM = pltpu.VMEM
F32 = jnp.float32
BF16 = jnp.bfloat16


def place(x, z, c):
    return (x * ZS + z) * CORES + c


def moves(rule):
    out = []
    for x in range(XS):
        for z in range(ZS):
            for c in range(CORES):
                out.append((place(x, z, c), place(*rule(x, z, c))))
    return out


def move(array, rule):
    return lax.ppermute(array, "tm", moves(rule))


def along_x(distance):
    return lambda x, z, c: ((x + distance) % XS, z, c)


def far_z(x, z, c):
    return x, z ^ 2, c


def near_z(x, z, c):
    return x, z ^ 1, c


def other_core(x, z, c):
    return x, z, 1 - c


def halo_of(tail):
    pairs = [(i, i + 1) for i in range(XS * ZS * CORES - 1)]
    return lax.ppermute(tail, "tm", pairs)


def trig_table():
    k = np.arange(FOUT)[:, None]
    n = np.arange(FINE)[None, :]
    phase = (k * n % FINE) * (2.0 * np.pi / FINE)
    c, s = np.cos(phase), np.sin(phase)
    real_row = np.stack([c, s], -1).reshape(FOUT, 2 * FINE)
    imag_row = np.stack([-s, c], -1).reshape(FOUT, 2 * FINE)
    rows = np.stack([real_row, imag_row], 1).reshape(2 * FOUT, 2 * FINE)
    return np.tile(rows.astype(np.float32), (1, 2 * BLOCK))


def spec(n):
    return [pl.BlockSpec(memory_space=VMEM)] * n


def shape(*dims, kind=BF16):
    return jax.ShapeDtypeStruct(dims, kind)


def band_matrix(taps_ref, trig_ref, band_ref):
    me = lax.axis_index("tm")
    x = me // (ZS * CORES)
    odd = me // 4 % 2
    width = 2 * WINDOW
    taps_len = TAPS * FINE
    row = lax.broadcasted_iota(jnp.int32, (taps_len, width), 0)
    col = lax.broadcasted_iota(jnp.int32, (taps_len, width), 1)
    pick = (col // 2 == row).astype(F32)
    taps = jnp.broadcast_to(taps_ref[...], (BLOCK, taps_len))
    twice = lax.dot_general(
        taps, pick, (((1,), (0,)), ((), ())), precision=lax.Precision.HIGHEST, preferred_element_type=F32
    )
    frame = lax.broadcasted_iota(jnp.int32, (BLOCK, width), 0)
    shifted = jnp.zeros((BLOCK, width), F32)
    for f in range(BLOCK):
        shifted = jnp.where(frame == f, pltpu.roll(twice, 2 * FINE * (f + 1) % width, 1), shifted)
    for d in range(XS):
        for other in range(2):
            k = (x + d) % XS * 2 + (odd + other) % 2
            for ro in range(2):
                at = ((d * 2 + other) * 2 + ro) * BLOCK
                wave = trig_ref[pl.ds(k * 2 + ro, 1), :]
                band_ref[at : at + BLOCK, :] = (shifted * wave).astype(BF16)


def tail_copy(volt_ref, out_ref, sem):
    n = out_ref.shape[0]
    copy = pltpu.make_async_copy(volt_ref.at[pl.ds(volt_ref.shape[0] - n, n)], out_ref, sem)
    copy.start()
    copy.wait()


def filter_late(taps_ref, trig_ref, volt_ref, band_ref, *out_refs):
    band_matrix(taps_ref, trig_ref, band_ref)
    for i in range(2):
        start = i * BLOCK * FINE
        window = volt_ref[start : start + WINDOW].reshape(2 * WINDOW, S)
        out = jnp.dot(band_ref[...], window, preferred_element_type=F32).astype(BF16)
        for d in range(XS):
            for other in range(2):
                at = (2 * other + i) * ROWS
                out_refs[d][at : at + ROWS, :] = out[(2 * d + other) * ROWS : (2 * d + other + 1) * ROWS]


def filter_first(halo_ref, volt_ref, band_ref, *out_refs):
    here = BLOCK * FINE
    own = volt_ref[0:here].reshape(2 * here, S)
    prior = halo_ref[...].reshape(2 * here - 2 * FINE, S)
    band = band_ref[...]
    out = jnp.dot(band[:, 2 * here :], own, preferred_element_type=F32)
    out += jnp.dot(band[:, 2 * FINE : 2 * here], prior, preferred_element_type=F32)
    out = out.astype(BF16)
    for d in range(XS):
        out_refs[d][...] = out[2 * d * ROWS : 2 * (d + 1) * ROWS]


def products(n_pieces, scale, *refs):
    pieces, rest = refs[:n_pieces], refs[n_pieces:]
    out_ref = rest[-1]
    j = pl.program_id(0)
    quarter = lax.axis_index("tm") % 4
    cols = pl.ds(pl.multiple_of(quarter * 256, 256), 256)
    rows = pl.ds(pl.multiple_of(j * 256, 256), 256)
    total = None
    for piece in pieces:
        n = piece.shape[0]
        here = piece[:, cols]
        halves = here.reshape(n // ROWS, 2, BLOCK, 256)
        turned = jnp.stack([halves[:, 1], -halves[:, 0]], 1).reshape(n, 256)
        both = jnp.concatenate([here, turned], 1)
        part = lax.dot_general(
            piece[:, rows], both, (((0,), (0,)), ((), ())), preferred_element_type=F32
        )
        total = part if total is None else total + part
    real, imag = total[:, :256], total[:, 256:]
    if len(rest) > 1:
        real += rest[0][0]
        imag += rest[0][1]
    if scale is not None:
        real, imag = real * scale, imag * scale
    out_ref[0] = real
    out_ref[1] = imag


def correlate(pieces, acc, scale=None):
    frames = sum(p.shape[0] for p in pieces)
    block = pl.BlockSpec((2, 256, 256), lambda j: (0, j, 0))
    more = [] if acc is None else [acc]
    return pl.pallas_call(
        functools.partial(products, len(pieces), scale),
        grid=(4,),
        out_shape=shape(2, S, 256, kind=F32),
        in_specs=[pl.BlockSpec(p.shape, lambda j: (0, 0), memory_space=VMEM, pipeline_mode=pl.Buffered(1)) for p in pieces]
        + [block] * len(more),
        out_specs=block,
        compiler_params=pltpu.CompilerParams(vmem_limit_bytes=40 << 20),
        cost_estimate=pl.CostEstimate(flops=2 * frames * S * 512, bytes_accessed=4 << 20, transcendentals=0),
    )(*pieces, *more)


def spread(slabs):
    return [slabs[0]] + [move(slabs[d], along_x(d)) for d in range(1, XS)]


def part(slabs, other):
    half = slabs[0].shape[0] // 2
    return jnp.concatenate([slab[other * half : (other + 1) * half] for slab in slabs], 0)


def shards(voltage, taps):
    samples_here = voltage.shape[0]
    volt = voltage.reshape(samples_here, 2, S)
    params = pltpu.CompilerParams(vmem_limit_bytes=40 << 20)
    tail = pl.pallas_call(
        tail_copy,
        out_shape=shape((TAPS - 1) * FINE, 2, S),
        in_specs=[pl.BlockSpec(memory_space=VMEM)],
        out_specs=pl.BlockSpec(memory_space=VMEM),
        scratch_shapes=[pltpu.SemaphoreType.DMA],
        compiler_params=params,
    )(volt)
    halo = halo_of(tail)
    band, *late_out = pl.pallas_call(
        filter_late,
        out_shape=(shape(4 * FOUT * BLOCK // 2, 2 * WINDOW), *[shape(4 * ROWS, S)] * XS),
        in_specs=spec(3),
        out_specs=spec(1 + XS),
        compiler_params=params,
        cost_estimate=pl.CostEstimate(flops=2 << 29, bytes_accessed=6 << 20, transcendentals=0),
    )(taps.reshape(1, -1), jnp.asarray(trig_table()), volt)
    late_all = spread(late_out)
    halo, *late_all = lax.optimization_barrier((halo, *late_all))
    first_out = pl.pallas_call(
        filter_first,
        out_shape=[shape(2 * ROWS, S)] * XS,
        in_specs=spec(3),
        out_specs=spec(XS),
        compiler_params=params,
        cost_estimate=pl.CostEstimate(flops=1 << 29, bytes_accessed=3 << 20, transcendentals=0),
    )(halo, volt, band)
    ta = move(part(late_all, 1), far_z)
    ma = part(late_all, 0)
    ma_near = move(ma, near_z)
    first_all = spread(first_out)
    tb = move(part(first_all, 1), far_z)
    ta_near = move(ta, near_z)
    b_own = jnp.concatenate([part(first_all, 0), tb], 0)
    b_near = move(b_own, near_z)
    ma = jnp.concatenate([ma, ma_near], 0)
    acc = correlate([ma, move(ma, other_core)], None)
    acc, ta_near, b_near = lax.optimization_barrier((acc, ta_near, b_near))
    near = jnp.concatenate([ta_near, b_near], 0)
    near_core = move(near, other_core)
    own = jnp.concatenate([ta, b_own], 0)
    acc = correlate([own, move(own, other_core)], acc)
    pieces = [near, near_core]
    frames = samples_here // FINE * XS * ZS * CORES
    return correlate(pieces, acc, 1.0 / frames)[None]


def solution(mesh):
    in_specs = (P("tm", None, "chan", None), P())
    out_specs = P("chan", None, None, "tm")
    return jax.shard_map(shards, mesh=mesh, in_specs=in_specs, out_specs=out_specs, check_vma=False)
```

```python
import functools

import jax
import jax.numpy as jnp
import numpy as np
from jax import lax
from jax.experimental import pallas as pl
from jax.experimental.pallas import tpu as pltpu
from jax.sharding import PartitionSpec as P

FINE = 16
FOUT = 8
TAPS = 16
S = 1024
XS, ZS, CORES = 4, 4, 2
BLOCK = 16
ROWS = 2 * BLOCK
WINDOW = 2 * BLOCK * FINE
VMEM = pltpu.VMEM
F32 = jnp.float32
BF16 = jnp.bfloat16


def place(x, z, c):
    return (x * ZS + z) * CORES + c


def moves(rule):
    out = []
    for x in range(XS):
        for z in range(ZS):
            for c in range(CORES):
                out.append((place(x, z, c), place(*rule(x, z, c))))
    return out


def move(array, rule):
    return lax.ppermute(array, "tm", moves(rule))


def along_x(distance):
    return lambda x, z, c: ((x + distance) % XS, z, c)


def far_z(x, z, c):
    return x, z ^ 2, c


def near_z(x, z, c):
    return x, z ^ 1, c


def other_core(x, z, c):
    return x, z, 1 - c


def halo_of(tail):
    pairs = [(i, i + 1) for i in range(XS * ZS * CORES - 1)]
    return lax.ppermute(tail, "tm", pairs)


def trig_table():
    k = np.arange(FOUT)[:, None]
    n = np.arange(FINE)[None, :]
    phase = (k * n % FINE) * (2.0 * np.pi / FINE)
    c, s = np.cos(phase), np.sin(phase)
    real_row = np.stack([c, s], -1).reshape(FOUT, 2 * FINE)
    imag_row = np.stack([-s, c], -1).reshape(FOUT, 2 * FINE)
    rows = np.stack([real_row, imag_row], 1).reshape(2 * FOUT, 2 * FINE)
    return np.tile(rows.astype(np.float32), (1, 2 * BLOCK))


def spec(n):
    return [pl.BlockSpec(memory_space=VMEM)] * n


def shape(*dims, kind=BF16):
    return jax.ShapeDtypeStruct(dims, kind)


def band_matrix(taps_ref, trig_ref, band_ref):
    me = lax.axis_index("tm")
    x = me // (ZS * CORES)
    odd = me // 4 % 2
    width = 2 * WINDOW
    taps_len = TAPS * FINE
    row = lax.broadcasted_iota(jnp.int32, (taps_len, width), 0)
    col = lax.broadcasted_iota(jnp.int32, (taps_len, width), 1)
    pick = (col // 2 == row).astype(F32)
    taps = jnp.broadcast_to(taps_ref[...], (BLOCK, taps_len))
    twice = lax.dot_general(
        taps, pick, (((1,), (0,)), ((), ())), precision=lax.Precision.HIGHEST, preferred_element_type=F32
    )
    frame = lax.broadcasted_iota(jnp.int32, (BLOCK, width), 0)
    shifted = jnp.zeros((BLOCK, width), F32)
    for f in range(BLOCK):
        shifted = jnp.where(frame == f, pltpu.roll(twice, 2 * FINE * (f + 1) % width, 1), shifted)
    for d in range(XS):
        for other in range(2):
            k = (x + d) % XS * 2 + (odd + other) % 2
            for ro in range(2):
                at = ((d * 2 + other) * 2 + ro) * BLOCK
                wave = trig_ref[pl.ds(k * 2 + ro, 1), :]
                band_ref[at : at + BLOCK, :] = (shifted * wave).astype(BF16)


def tail_copy(volt_ref, out_ref, sem):
    n = out_ref.shape[0]
    copy = pltpu.make_async_copy(volt_ref.at[pl.ds(volt_ref.shape[0] - n, n)], out_ref, sem)
    copy.start()
    copy.wait()


def filter_late(taps_ref, trig_ref, volt_ref, band_ref, *out_refs):
    band_matrix(taps_ref, trig_ref, band_ref)
    for i in range(2):
        start = i * BLOCK * FINE
        window = volt_ref[start : start + WINDOW].reshape(2 * WINDOW, S)
        out = jnp.dot(band_ref[...], window, preferred_element_type=F32).astype(BF16)
        for d in range(XS):
            for other in range(2):
                at = (2 * other + i) * ROWS
                out_refs[d][at : at + ROWS, :] = out[(2 * d + other) * ROWS : (2 * d + other + 1) * ROWS]


def filter_first(halo_ref, volt_ref, band_ref, *out_refs):
    here = BLOCK * FINE
    own = volt_ref[0:here].reshape(2 * here, S)
    prior = halo_ref[...].reshape(2 * here - 2 * FINE, S)
    band = band_ref[...]
    out = jnp.dot(band[:, 2 * here :], own, preferred_element_type=F32)
    out += jnp.dot(band[:, 2 * FINE : 2 * here], prior, preferred_element_type=F32)
    out = out.astype(BF16)
    for d in range(XS):
        out_refs[d][...] = out[2 * d * ROWS : 2 * (d + 1) * ROWS]


def products(n_pieces, scale, *refs):
    pieces, rest = refs[:n_pieces], refs[n_pieces:]
    out_ref = rest[-1]
    j = pl.program_id(0)
    quarter = lax.axis_index("tm") % 4
    cols = pl.ds(pl.multiple_of(quarter * 256, 256), 256)
    rows = pl.ds(pl.multiple_of(j * 256, 256), 256)
    total = None
    for piece in pieces:
        n = piece.shape[0]
        here = piece[:, cols]
        halves = here.reshape(n // ROWS, 2, BLOCK, 256)
        turned = jnp.stack([halves[:, 1], -halves[:, 0]], 1).reshape(n, 256)
        both = jnp.concatenate([here, turned], 1)
        part = lax.dot_general(
            piece[:, rows], both, (((0,), (0,)), ((), ())), preferred_element_type=F32
        )
        total = part if total is None else total + part
    real, imag = total[:, :256], total[:, 256:]
    if len(rest) > 1:
        real += rest[0][0]
        imag += rest[0][1]
    if scale is not None:
        real, imag = real * scale, imag * scale
    out_ref[0] = real
    out_ref[1] = imag


def correlate(pieces, acc, scale=None):
    frames = sum(p.shape[0] for p in pieces)
    block = pl.BlockSpec((2, 256, 256), lambda j: (0, j, 0))
    more = [] if acc is None else [acc]
    return pl.pallas_call(
        functools.partial(products, len(pieces), scale),
        grid=(4,),
        out_shape=shape(2, S, 256, kind=F32),
        in_specs=[pl.BlockSpec(p.shape, lambda j: (0, 0), memory_space=VMEM, pipeline_mode=pl.Buffered(1)) for p in pieces]
        + [block] * len(more),
        out_specs=block,
        compiler_params=pltpu.CompilerParams(vmem_limit_bytes=40 << 20),
        cost_estimate=pl.CostEstimate(flops=2 * frames * S * 512, bytes_accessed=4 << 20, transcendentals=0),
    )(*pieces, *more)


def spread(slabs):
    return [slabs[0]] + [move(slabs[d], along_x(d)) for d in range(1, XS)]


def part(slabs, other):
    half = slabs[0].shape[0] // 2
    return jnp.concatenate([slab[other * half : (other + 1) * half] for slab in slabs], 0)


def shards(voltage, taps):
    samples_here = voltage.shape[0]
    volt = voltage.reshape(samples_here, 2, S)
    params = pltpu.CompilerParams(vmem_limit_bytes=40 << 20)
    tail = pl.pallas_call(
        tail_copy,
        out_shape=shape((TAPS - 1) * FINE, 2, S),
        in_specs=[pl.BlockSpec(memory_space=VMEM)],
        out_specs=pl.BlockSpec(memory_space=VMEM),
        scratch_shapes=[pltpu.SemaphoreType.DMA],
        compiler_params=params,
    )(volt)
    halo = halo_of(tail)
    band, *late_out = pl.pallas_call(
        filter_late,
        out_shape=(shape(4 * FOUT * BLOCK // 2, 2 * WINDOW), *[shape(4 * ROWS, S)] * XS),
        in_specs=spec(3),
        out_specs=spec(1 + XS),
        compiler_params=params,
        cost_estimate=pl.CostEstimate(flops=2 << 29, bytes_accessed=6 << 20, transcendentals=0),
    )(taps.reshape(1, -1), jnp.asarray(trig_table()), volt)
    late_all = spread(late_out)
    halo, *late_all = lax.optimization_barrier((halo, *late_all))
    first_out = pl.pallas_call(
        filter_first,
        out_shape=[shape(2 * ROWS, S)] * XS,
        in_specs=spec(3),
        out_specs=spec(XS),
        compiler_params=params,
        cost_estimate=pl.CostEstimate(flops=1 << 29, bytes_accessed=3 << 20, transcendentals=0),
    )(halo, volt, band)
    ta = move(part(late_all, 1), far_z)
    ma = part(late_all, 0)
    ma_near = move(ma, near_z)
    first_all = spread(first_out)
    ma_near, *first_all = lax.optimization_barrier((ma_near, *first_all))
    mb, tb = part(first_all, 0), part(first_all, 1)
    mb_near, mb_rest = move(mb[: 4 * ROWS], near_z), mb[:0]
    tb, tb_rest = move(tb[: 4 * ROWS], far_z), tb[:0]
    ta, mb_near = lax.optimization_barrier((ta, mb_near))
    ta_near = move(ta, near_z)
    tb = jnp.concatenate([tb, tb_rest], 0)
    tb_near = move(tb, near_z)
    ma = jnp.concatenate([ma, ma_near], 0)
    acc = correlate([ma, move(ma, other_core)], None)
    acc, ta_near, tb_near = lax.optimization_barrier((acc, ta_near, tb_near))
    near = jnp.concatenate([ta_near, tb_near, tb], 0)
    near_core = move(near, other_core)
    own = jnp.concatenate([ta, mb, mb_near, mb_rest], 0)
    acc = correlate([own, move(own, other_core)], acc)
    pieces = [near, near_core]
    frames = samples_here // FINE * XS * ZS * CORES
    return correlate(pieces, acc, 1.0 / frames)[None]


def solution(mesh):
    in_specs = (P("tm", None, "chan", None), P())
    out_specs = P("chan", None, None, "tm")
    return jax.shard_map(shards, mesh=mesh, in_specs=in_specs, out_specs=out_specs, check_vma=False)
```

```python
import functools

import jax
import jax.numpy as jnp
import numpy as np
from jax import lax
from jax.experimental import pallas as pl
from jax.experimental.pallas import tpu as pltpu
from jax.sharding import PartitionSpec as P

FINE = 16
FOUT = 8
TAPS = 16
S = 1024
XS, ZS, CORES = 4, 4, 2
BLOCK = 16
ROWS = 2 * BLOCK
WINDOW = 2 * BLOCK * FINE
VMEM = pltpu.VMEM
F32 = jnp.float32
BF16 = jnp.bfloat16


def place(x, z, c):
    return (x * ZS + z) * CORES + c


def moves(rule):
    out = []
    for x in range(XS):
        for z in range(ZS):
            for c in range(CORES):
                out.append((place(x, z, c), place(*rule(x, z, c))))
    return out


def move(array, rule):
    return lax.ppermute(array, "tm", moves(rule))


def along_x(distance):
    return lambda x, z, c: ((x + distance) % XS, z, c)


def far_z(x, z, c):
    return x, z ^ 2, c


def near_z(x, z, c):
    return x, z ^ 1, c


def other_core(x, z, c):
    return x, z, 1 - c


def halo_of(tail):
    run = ZS * CORES
    pairs = [(i, i + 1) for i in range(XS * run - 1)]
    inside = [pair for pair in pairs if pair[1] % run]
    across = [pair for pair in pairs if not pair[1] % run]
    return lax.ppermute(tail, "tm", inside), lax.ppermute(tail, "tm", across)


def trig_table():
    k = np.arange(FOUT)[:, None]
    n = np.arange(FINE)[None, :]
    phase = (k * n % FINE) * (2.0 * np.pi / FINE)
    c, s = np.cos(phase), np.sin(phase)
    real_row = np.stack([c, s], -1).reshape(FOUT, 2 * FINE)
    imag_row = np.stack([-s, c], -1).reshape(FOUT, 2 * FINE)
    rows = np.stack([real_row, imag_row], 1).reshape(2 * FOUT, 2 * FINE)
    return np.tile(rows.astype(np.float32), (1, 2 * BLOCK))


def spec(n):
    return [pl.BlockSpec(memory_space=VMEM)] * n


def shape(*dims, kind=BF16):
    return jax.ShapeDtypeStruct(dims, kind)


def band_matrix(taps_ref, trig_ref, band_ref):
    me = lax.axis_index("tm")
    x = me // (ZS * CORES)
    odd = me // 4 % 2
    width = 2 * WINDOW
    taps_len = TAPS * FINE
    row = lax.broadcasted_iota(jnp.int32, (taps_len, width), 0)
    col = lax.broadcasted_iota(jnp.int32, (taps_len, width), 1)
    pick = (col // 2 == row).astype(F32)
    taps = jnp.broadcast_to(taps_ref[...], (BLOCK, taps_len))
    twice = lax.dot_general(
        taps, pick, (((1,), (0,)), ((), ())), precision=lax.Precision.HIGHEST, preferred_element_type=F32
    )
    frame = lax.broadcasted_iota(jnp.int32, (BLOCK, width), 0)
    shifted = jnp.zeros((BLOCK, width), F32)
    for f in range(BLOCK):
        shifted = jnp.where(frame == f, pltpu.roll(twice, 2 * FINE * (f + 1) % width, 1), shifted)
    for d in range(XS):
        for other in range(2):
            k = (x + d) % XS * 2 + (odd + other) % 2
            for ro in range(2):
                at = ((d * 2 + other) * 2 + ro) * BLOCK
                wave = trig_ref[pl.ds(k * 2 + ro, 1), :]
                band_ref[at : at + BLOCK, :] = (shifted * wave).astype(BF16)


def tail_copy(volt_ref, out_ref, sem):
    n = out_ref.shape[0]
    copy = pltpu.make_async_copy(volt_ref.at[pl.ds(volt_ref.shape[0] - n, n)], out_ref, sem)
    copy.start()
    copy.wait()


def filter_late(taps_ref, trig_ref, volt_ref, band_ref, *out_refs):
    band_matrix(taps_ref, trig_ref, band_ref)
    for i in range(2):
        start = i * BLOCK * FINE
        window = volt_ref[start : start + WINDOW].reshape(2 * WINDOW, S)
        out = jnp.dot(band_ref[...], window, preferred_element_type=F32).astype(BF16)
        for d in range(XS):
            for other in range(2):
                at = (2 * other + i) * ROWS
                out_refs[d][at : at + ROWS, :] = out[(2 * d + other) * ROWS : (2 * d + other + 1) * ROWS]


def filter_first(halo_ref, wrap_ref, volt_ref, band_ref, *out_refs):
    here = BLOCK * FINE
    own = volt_ref[0:here].reshape(2 * here, S)
    prior = (halo_ref[...] + wrap_ref[...]).reshape(2 * here - 2 * FINE, S)
    band = band_ref[...]
    out = jnp.dot(band[:, 2 * here :], own, preferred_element_type=F32)
    out += jnp.dot(band[:, 2 * FINE : 2 * here], prior, preferred_element_type=F32)
    out = out.astype(BF16)
    for d in range(XS):
        out_refs[d][...] = out[2 * d * ROWS : 2 * (d + 1) * ROWS]


def products(n_pieces, scale, *refs):
    pieces, rest = refs[:n_pieces], refs[n_pieces:]
    out_ref = rest[-1]
    j = pl.program_id(0)
    quarter = lax.axis_index("tm") % 4
    cols = pl.ds(pl.multiple_of(quarter * 256, 256), 256)
    rows = pl.ds(pl.multiple_of(j * 256, 256), 256)
    total = None
    for piece in pieces:
        n = piece.shape[0]
        here = piece[:, cols]
        halves = here.reshape(n // ROWS, 2, BLOCK, 256)
        turned = jnp.stack([halves[:, 1], -halves[:, 0]], 1).reshape(n, 256)
        both = jnp.concatenate([here, turned], 1)
        part = lax.dot_general(
            piece[:, rows], both, (((0,), (0,)), ((), ())), preferred_element_type=F32
        )
        total = part if total is None else total + part
    real, imag = total[:, :256], total[:, 256:]
    if len(rest) > 1:
        real += rest[0][0]
        imag += rest[0][1]
    if scale is not None:
        real, imag = real * scale, imag * scale
    out_ref[0] = real
    out_ref[1] = imag


def correlate(pieces, acc, scale=None):
    frames = sum(p.shape[0] for p in pieces)
    block = pl.BlockSpec((2, 256, 256), lambda j: (0, j, 0))
    more = [] if acc is None else [acc]
    return pl.pallas_call(
        functools.partial(products, len(pieces), scale),
        grid=(4,),
        out_shape=shape(2, S, 256, kind=F32),
        in_specs=[pl.BlockSpec(p.shape, lambda j: (0, 0), memory_space=VMEM, pipeline_mode=pl.Buffered(1)) for p in pieces]
        + [block] * len(more),
        out_specs=block,
        compiler_params=pltpu.CompilerParams(vmem_limit_bytes=40 << 20),
        cost_estimate=pl.CostEstimate(flops=2 * frames * S * 512, bytes_accessed=4 << 20, transcendentals=0),
    )(*pieces, *more)


def spread(slabs):
    return [slabs[0]] + [move(slabs[d], along_x(d)) for d in range(1, XS)]


def part(slabs, other):
    half = slabs[0].shape[0] // 2
    return jnp.concatenate([slab[other * half : (other + 1) * half] for slab in slabs], 0)


def shards(voltage, taps):
    samples_here = voltage.shape[0]
    volt = voltage.reshape(samples_here, 2, S)
    params = pltpu.CompilerParams(vmem_limit_bytes=40 << 20)
    tail = pl.pallas_call(
        tail_copy,
        out_shape=shape((TAPS - 1) * FINE, 2, S),
        in_specs=[pl.BlockSpec(memory_space=VMEM)],
        out_specs=pl.BlockSpec(memory_space=VMEM),
        scratch_shapes=[pltpu.SemaphoreType.DMA],
        compiler_params=params,
    )(volt)
    halo, wrap = halo_of(tail)
    band, *late_out = pl.pallas_call(
        filter_late,
        out_shape=(shape(4 * FOUT * BLOCK // 2, 2 * WINDOW), *[shape(4 * ROWS, S)] * XS),
        in_specs=spec(3),
        out_specs=spec(1 + XS),
        compiler_params=params,
        cost_estimate=pl.CostEstimate(flops=2 << 29, bytes_accessed=6 << 20, transcendentals=0),
    )(taps.reshape(1, -1), jnp.asarray(trig_table()), volt)
    late_all = spread(late_out)
    halo, *late_all = lax.optimization_barrier((halo, *late_all))
    first_out = pl.pallas_call(
        filter_first,
        out_shape=[shape(2 * ROWS, S)] * XS,
        in_specs=spec(4),
        out_specs=spec(XS),
        compiler_params=params,
        cost_estimate=pl.CostEstimate(flops=1 << 29, bytes_accessed=3 << 20, transcendentals=0),
    )(halo, wrap, volt, band)
    ta = move(part(late_all, 1), far_z)
    ma = part(late_all, 0)
    ma_near = move(ma, near_z)
    first_all = spread(first_out)
    tb = move(part(first_all, 1), far_z)
    ta_near = move(ta, near_z)
    b_own = jnp.concatenate([part(first_all, 0), tb], 0)
    b_near = move(b_own, near_z)
    ma = jnp.concatenate([ma, ma_near], 0)
    acc = correlate([ma, move(ma, other_core)], None)
    acc, ta_near, b_near = lax.optimization_barrier((acc, ta_near, b_near))
    near = jnp.concatenate([ta_near, b_near], 0)
    near_core = move(near, other_core)
    own = jnp.concatenate([ta, b_own], 0)
    acc = correlate([own, move(own, other_core)], acc)
    pieces = [near, near_core]
    frames = samples_here // FINE * XS * ZS * CORES
    return correlate(pieces, acc, 1.0 / frames)[None]


def solution(mesh):
    in_specs = (P("tm", None, "chan", None), P())
    out_specs = P("chan", None, None, "tm")
    return jax.shard_map(shards, mesh=mesh, in_specs=in_specs, out_specs=out_specs, check_vma=False)
```

```python
import functools

import jax
import jax.numpy as jnp
import numpy as np
from jax import lax
from jax.experimental import pallas as pl
from jax.experimental.pallas import tpu as pltpu
from jax.sharding import PartitionSpec as P

FINE = 16
FOUT = 8
TAPS = 16
S = 1024
XS, ZS, CORES = 4, 4, 2
BLOCK = 16
ROWS = 2 * BLOCK
WINDOW = 2 * BLOCK * FINE
VMEM = pltpu.VMEM
F32 = jnp.float32
BF16 = jnp.bfloat16


def place(x, z, c):
    return (x * ZS + z) * CORES + c


def moves(rule):
    out = []
    for x in range(XS):
        for z in range(ZS):
            for c in range(CORES):
                out.append((place(x, z, c), place(*rule(x, z, c))))
    return out


def move(array, rule):
    return lax.ppermute(array, "tm", moves(rule))


def along_x(distance):
    return lambda x, z, c: ((x + distance) % XS, z, c)


def far_z(x, z, c):
    return x, z ^ 2, c


def near_z(x, z, c):
    return x, z ^ 1, c


def other_core(x, z, c):
    return x, z, 1 - c


def halo_of(tail):
    run = ZS * CORES
    pairs = [(i, i + 1) for i in range(XS * run - 1)]
    inside = [pair for pair in pairs if pair[1] % run]
    across = [pair for pair in pairs if not pair[1] % run]
    return lax.ppermute(tail, "tm", inside), lax.ppermute(tail, "tm", across)


def trig_table():
    k = np.arange(FOUT)[:, None]
    n = np.arange(FINE)[None, :]
    phase = (k * n % FINE) * (2.0 * np.pi / FINE)
    c, s = np.cos(phase), np.sin(phase)
    real_row = np.stack([c, s], -1).reshape(FOUT, 2 * FINE)
    imag_row = np.stack([-s, c], -1).reshape(FOUT, 2 * FINE)
    rows = np.stack([real_row, imag_row], 1).reshape(2 * FOUT, 2 * FINE)
    return np.tile(rows.astype(np.float32), (1, 2 * BLOCK))


def spec(n):
    return [pl.BlockSpec(memory_space=VMEM)] * n


def shape(*dims, kind=BF16):
    return jax.ShapeDtypeStruct(dims, kind)


def band_matrix(taps_ref, trig_ref, band_ref):
    me = lax.axis_index("tm")
    x = me // (ZS * CORES)
    odd = me // 4 % 2
    width = 2 * WINDOW
    taps_len = TAPS * FINE
    row = lax.broadcasted_iota(jnp.int32, (taps_len, width), 0)
    col = lax.broadcasted_iota(jnp.int32, (taps_len, width), 1)
    pick = (col // 2 == row).astype(F32)
    taps = jnp.broadcast_to(taps_ref[...], (BLOCK, taps_len))
    twice = lax.dot_general(
        taps, pick, (((1,), (0,)), ((), ())), precision=lax.Precision.HIGHEST, preferred_element_type=F32
    )
    frame = lax.broadcasted_iota(jnp.int32, (BLOCK, width), 0)
    shifted = jnp.zeros((BLOCK, width), F32)
    for f in range(BLOCK):
        shifted = jnp.where(frame == f, pltpu.roll(twice, 2 * FINE * (f + 1) % width, 1), shifted)
    for d in range(XS):
        for other in range(2):
            k = (x + d) % XS * 2 + (odd + other) % 2
            for ro in range(2):
                at = ((d * 2 + other) * 2 + ro) * BLOCK
                wave = trig_ref[pl.ds(k * 2 + ro, 1), :]
                band_ref[at : at + BLOCK, :] = (shifted * wave).astype(BF16)


def tail_copy(volt_ref, out_ref, sem):
    n = out_ref.shape[0]
    copy = pltpu.make_async_copy(volt_ref.at[pl.ds(volt_ref.shape[0] - n, n)], out_ref, sem)
    copy.start()
    copy.wait()


def filter_late(taps_ref, trig_ref, volt_ref, band_ref, *out_refs):
    band_matrix(taps_ref, trig_ref, band_ref)
    for i in range(2):
        start = i * BLOCK * FINE
        window = volt_ref[start : start + WINDOW].reshape(2 * WINDOW, S)
        out = jnp.dot(band_ref[...], window, preferred_element_type=F32).astype(BF16)
        for d in range(XS):
            for other in range(2):
                at = (2 * other + i) * ROWS
                out_refs[d][at : at + ROWS, :] = out[(2 * d + other) * ROWS : (2 * d + other + 1) * ROWS]


def filter_first(halo_ref, wrap_ref, volt_ref, band_ref, *out_refs):
    here = BLOCK * FINE
    own = volt_ref[0:here].reshape(2 * here, S)
    prior = (halo_ref[...] + wrap_ref[...]).reshape(2 * here - 2 * FINE, S)
    band = band_ref[...]
    out = jnp.dot(band[:, 2 * here :], own, preferred_element_type=F32)
    out += jnp.dot(band[:, 2 * FINE : 2 * here], prior, preferred_element_type=F32)
    out = out.astype(BF16)
    for d in range(XS):
        out_refs[d][...] = out[2 * d * ROWS : 2 * (d + 1) * ROWS]


def products(n_pieces, scale, *refs):
    pieces, rest = refs[:n_pieces], refs[n_pieces:]
    out_ref = rest[-1]
    j = pl.program_id(0)
    quarter = lax.axis_index("tm") % 4
    cols = pl.ds(pl.multiple_of(quarter * 256, 256), 256)
    rows = pl.ds(pl.multiple_of(j * 256, 256), 256)
    total = None
    for piece in pieces:
        n = piece.shape[0]
        here = piece[:, cols]
        halves = here.reshape(n // ROWS, 2, BLOCK, 256)
        turned = jnp.stack([halves[:, 1], -halves[:, 0]], 1).reshape(n, 256)
        both = jnp.concatenate([here, turned], 1)
        part = lax.dot_general(
            piece[:, rows], both, (((0,), (0,)), ((), ())), preferred_element_type=F32
        )
        total = part if total is None else total + part
    real, imag = total[:, :256], total[:, 256:]
    if len(rest) > 1:
        real += rest[0][0]
        imag += rest[0][1]
    if scale is not None:
        real, imag = real * scale, imag * scale
    out_ref[0] = real
    out_ref[1] = imag


def correlate(pieces, acc, scale=None):
    frames = sum(p.shape[0] for p in pieces)
    block = pl.BlockSpec((2, 256, 256), lambda j: (0, j, 0))
    more = [] if acc is None else [acc]
    return pl.pallas_call(
        functools.partial(products, len(pieces), scale),
        grid=(4,),
        out_shape=shape(2, S, 256, kind=F32),
        in_specs=[pl.BlockSpec(p.shape, lambda j: (0, 0), memory_space=VMEM, pipeline_mode=pl.Buffered(1)) for p in pieces]
        + [block] * len(more),
        out_specs=block,
        compiler_params=pltpu.CompilerParams(vmem_limit_bytes=40 << 20),
        cost_estimate=pl.CostEstimate(flops=2 * frames * S * 512, bytes_accessed=4 << 20, transcendentals=0),
    )(*pieces, *more)


def spread(slabs):
    return [slabs[0]] + [move(slabs[d], along_x(d)) for d in range(1, XS)]


def part(slabs, other):
    half = slabs[0].shape[0] // 2
    return jnp.concatenate([slab[other * half : (other + 1) * half] for slab in slabs], 0)


def shards(voltage, taps):
    samples_here = voltage.shape[0]
    volt = voltage.reshape(samples_here, 2, S)
    params = pltpu.CompilerParams(vmem_limit_bytes=40 << 20)
    tail = pl.pallas_call(
        tail_copy,
        out_shape=shape((TAPS - 1) * FINE, 2, S),
        in_specs=[pl.BlockSpec(memory_space=VMEM)],
        out_specs=pl.BlockSpec(memory_space=VMEM),
        scratch_shapes=[pltpu.SemaphoreType.DMA],
        compiler_params=params,
    )(volt)
    halo, wrap = halo_of(tail)
    band, *late_out = pl.pallas_call(
        filter_late,
        out_shape=(shape(4 * FOUT * BLOCK // 2, 2 * WINDOW), *[shape(4 * ROWS, S)] * XS),
        in_specs=spec(3),
        out_specs=spec(1 + XS),
        compiler_params=params,
        cost_estimate=pl.CostEstimate(flops=2 << 29, bytes_accessed=6 << 20, transcendentals=0),
    )(taps.reshape(1, -1), jnp.asarray(trig_table()), volt)
    late_all = spread(late_out)
    halo, *late_all = lax.optimization_barrier((halo, *late_all))
    first_out = pl.pallas_call(
        filter_first,
        out_shape=[shape(2 * ROWS, S)] * XS,
        in_specs=spec(4),
        out_specs=spec(XS),
        compiler_params=params,
        cost_estimate=pl.CostEstimate(flops=1 << 29, bytes_accessed=3 << 20, transcendentals=0),
    )(halo, wrap, volt, band)
    ta = move(part(late_all, 1), far_z)
    ma = part(late_all, 0)
    ma_near = move(ma, near_z)
    first_all = spread(first_out)
    mb = part(first_all, 0)
    tb = move(part(first_all, 1), far_z)
    ta_near = move(ta, near_z)
    b_near = move(jnp.concatenate([mb, tb], 0), near_z)
    ma = jnp.concatenate([ma, ma_near], 0)
    acc = correlate([ma, move(ma, other_core)], None)
    own = jnp.concatenate([ta, mb], 0)
    acc = correlate([own, move(own, other_core), ta_near], acc)
    ta_core = move(ta_near, other_core)
    acc, b_near, ta_core = lax.optimization_barrier((acc, b_near, ta_core))
    last = jnp.concatenate([b_near, tb], 0)
    pieces = [ta_core, last, move(last, other_core)]
    frames = samples_here // FINE * XS * ZS * CORES
    return correlate(pieces, acc, 1.0 / frames)[None]


def solution(mesh):
    in_specs = (P("tm", None, "chan", None), P())
    out_specs = P("chan", None, None, "tm")
    return jax.shard_map(shards, mesh=mesh, in_specs=in_specs, out_specs=out_specs, check_vma=False)
```

```python
import functools

import jax
import jax.numpy as jnp
import numpy as np
from jax import lax
from jax.experimental import pallas as pl
from jax.experimental.pallas import tpu as pltpu
from jax.sharding import PartitionSpec as P

FINE = 16
FOUT = 8
TAPS = 16
S = 1024
XS, ZS, CORES = 4, 4, 2
BLOCK = 16
ROWS = 2 * BLOCK
WINDOW = 2 * BLOCK * FINE
VMEM = pltpu.VMEM
F32 = jnp.float32
BF16 = jnp.bfloat16


def place(x, z, c):
    return (x * ZS + z) * CORES + c


def moves(rule):
    out = []
    for x in range(XS):
        for z in range(ZS):
            for c in range(CORES):
                out.append((place(x, z, c), place(*rule(x, z, c))))
    return out


def move(array, rule):
    return lax.ppermute(array, "tm", moves(rule))


def along_x(distance):
    return lambda x, z, c: ((x + distance) % XS, z, c)


def far_z(x, z, c):
    return x, z ^ 2, c


def near_z(x, z, c):
    return x, z ^ 1, c


def other_core(x, z, c):
    return x, z, 1 - c


def halo_of(tail):
    run = ZS * CORES
    pairs = [(i, i + 1) for i in range(XS * run - 1)]
    inside = [pair for pair in pairs if pair[1] % run]
    across = [pair for pair in pairs if not pair[1] % run]
    return lax.ppermute(tail, "tm", inside), lax.ppermute(tail, "tm", across)


def trig_table():
    k = np.arange(FOUT)[:, None]
    n = np.arange(FINE)[None, :]
    phase = (k * n % FINE) * (2.0 * np.pi / FINE)
    c, s = np.cos(phase), np.sin(phase)
    real_row = np.stack([c, s], -1).reshape(FOUT, 2 * FINE)
    imag_row = np.stack([-s, c], -1).reshape(FOUT, 2 * FINE)
    rows = np.stack([real_row, imag_row], 1).reshape(2 * FOUT, 2 * FINE)
    return np.tile(rows.astype(np.float32), (1, 2 * BLOCK))


def spec(n):
    return [pl.BlockSpec(memory_space=VMEM)] * n


def shape(*dims, kind=BF16):
    return jax.ShapeDtypeStruct(dims, kind)


def band_matrix(taps_ref, trig_ref, band_ref):
    me = lax.axis_index("tm")
    x = me // (ZS * CORES)
    odd = me // 4 % 2
    width = 2 * WINDOW
    taps_len = TAPS * FINE
    row = lax.broadcasted_iota(jnp.int32, (taps_len, width), 0)
    col = lax.broadcasted_iota(jnp.int32, (taps_len, width), 1)
    pick = (col // 2 == row).astype(F32)
    taps = jnp.broadcast_to(taps_ref[...], (BLOCK, taps_len))
    twice = lax.dot_general(
        taps, pick, (((1,), (0,)), ((), ())), precision=lax.Precision.HIGHEST, preferred_element_type=F32
    )
    frame = lax.broadcasted_iota(jnp.int32, (BLOCK, width), 0)
    shifted = jnp.zeros((BLOCK, width), F32)
    for f in range(BLOCK):
        shifted = jnp.where(frame == f, pltpu.roll(twice, 2 * FINE * (f + 1) % width, 1), shifted)
    for d in range(XS):
        for other in range(2):
            k = (x + d) % XS * 2 + (odd + other) % 2
            for ro in range(2):
                at = ((d * 2 + other) * 2 + ro) * BLOCK
                wave = trig_ref[pl.ds(k * 2 + ro, 1), :]
                band_ref[at : at + BLOCK, :] = (shifted * wave).astype(BF16)


def tail_copy(volt_ref, out_ref, sem):
    n = out_ref.shape[0]
    copy = pltpu.make_async_copy(volt_ref.at[pl.ds(volt_ref.shape[0] - n, n)], out_ref, sem)
    copy.start()
    copy.wait()


def filter_late(taps_ref, trig_ref, volt_ref, band_ref, *out_refs):
    band_matrix(taps_ref, trig_ref, band_ref)
    for i in range(2):
        start = i * BLOCK * FINE
        window = volt_ref[start : start + WINDOW].reshape(2 * WINDOW, S)
        out = jnp.dot(band_ref[...], window, preferred_element_type=F32).astype(BF16)
        for d in range(XS):
            for other in range(2):
                at = (2 * other + i) * ROWS
                out_refs[d][at : at + ROWS, :] = out[(2 * d + other) * ROWS : (2 * d + other + 1) * ROWS]


def filter_first(halo_ref, wrap_ref, volt_ref, band_ref, *out_refs):
    here = BLOCK * FINE
    own = volt_ref[0:here].reshape(2 * here, S)
    prior = (halo_ref[...] + wrap_ref[...]).reshape(2 * here - 2 * FINE, S)
    band = band_ref[...]
    out = jnp.dot(band[:, 2 * here :], own, preferred_element_type=F32)
    out += jnp.dot(band[:, 2 * FINE : 2 * here], prior, preferred_element_type=F32)
    out = out.astype(BF16)
    for d in range(XS):
        out_refs[d][...] = out[2 * d * ROWS : 2 * (d + 1) * ROWS]


def products(n_pieces, scale, *refs):
    pieces, rest = refs[:n_pieces], refs[n_pieces:]
    out_ref = rest[-1]
    j = pl.program_id(0)
    quarter = lax.axis_index("tm") % 4
    cols = pl.ds(pl.multiple_of(quarter * 256, 256), 256)
    rows = pl.ds(pl.multiple_of(j * 256, 256), 256)
    total = None
    for piece in pieces:
        n = piece.shape[0]
        here = piece[:, cols]
        halves = here.reshape(n // ROWS, 2, BLOCK, 256)
        turned = jnp.stack([halves[:, 1], -halves[:, 0]], 1).reshape(n, 256)
        both = jnp.concatenate([here, turned], 1)
        part = lax.dot_general(
            piece[:, rows], both, (((0,), (0,)), ((), ())), preferred_element_type=F32
        )
        total = part if total is None else total + part
    real, imag = total[:, :256], total[:, 256:]
    if len(rest) > 1:
        real += rest[0][0]
        imag += rest[0][1]
    if scale is not None:
        real, imag = real * scale, imag * scale
    out_ref[0] = real
    out_ref[1] = imag


def correlate(pieces, acc, scale=None):
    frames = sum(p.shape[0] for p in pieces)
    block = pl.BlockSpec((2, 256, 256), lambda j: (0, j, 0))
    more = [] if acc is None else [acc]
    return pl.pallas_call(
        functools.partial(products, len(pieces), scale),
        grid=(4,),
        out_shape=shape(2, S, 256, kind=F32),
        in_specs=[pl.BlockSpec(p.shape, lambda j: (0, 0), memory_space=VMEM, pipeline_mode=pl.Buffered(1)) for p in pieces]
        + [block] * len(more),
        out_specs=block,
        compiler_params=pltpu.CompilerParams(vmem_limit_bytes=40 << 20),
        cost_estimate=pl.CostEstimate(flops=2 * frames * S * 512, bytes_accessed=4 << 20, transcendentals=0),
    )(*pieces, *more)


def spread(slabs):
    return [slabs[0]] + [move(slabs[d], along_x(d)) for d in range(1, XS)]


def part(slabs, other):
    half = slabs[0].shape[0] // 2
    return jnp.concatenate([slab[other * half : (other + 1) * half] for slab in slabs], 0)


def shards(voltage, taps):
    samples_here = voltage.shape[0]
    volt = voltage.reshape(samples_here, 2, S)
    params = pltpu.CompilerParams(vmem_limit_bytes=40 << 20)
    tail = pl.pallas_call(
        tail_copy,
        out_shape=shape((TAPS - 1) * FINE, 2, S),
        in_specs=[pl.BlockSpec(memory_space=VMEM)],
        out_specs=pl.BlockSpec(memory_space=VMEM),
        scratch_shapes=[pltpu.SemaphoreType.DMA],
        compiler_params=params,
    )(volt)
    halo, wrap = halo_of(tail)
    band, *late_out = pl.pallas_call(
        filter_late,
        out_shape=(shape(4 * FOUT * BLOCK // 2, 2 * WINDOW), *[shape(4 * ROWS, S)] * XS),
        in_specs=spec(3),
        out_specs=spec(1 + XS),
        compiler_params=params,
        cost_estimate=pl.CostEstimate(flops=2 << 29, bytes_accessed=6 << 20, transcendentals=0),
    )(taps.reshape(1, -1), jnp.asarray(trig_table()), volt)
    late_all = spread(late_out)
    halo, *late_all = lax.optimization_barrier((halo, *late_all))
    first_out = pl.pallas_call(
        filter_first,
        out_shape=[shape(2 * ROWS, S)] * XS,
        in_specs=spec(4),
        out_specs=spec(XS),
        compiler_params=params,
        cost_estimate=pl.CostEstimate(flops=1 << 29, bytes_accessed=3 << 20, transcendentals=0),
    )(halo, wrap, volt, band)
    ta = move(part(late_all, 1), far_z)
    ma = part(late_all, 0)
    ma_near = move(ma, near_z)
    first_all = spread(first_out)
    mb = part(first_all, 0)
    tb = move(part(first_all, 1), far_z)
    ta_near = move(ta, near_z)
    b_near = move(jnp.concatenate([mb, tb], 0), near_z)
    ma = jnp.concatenate([ma, ma_near], 0)
    acc = correlate([ma, move(ma, other_core)], None)
    own = jnp.concatenate([ta, mb], 0)
    acc = correlate([own, move(own, other_core), ta_near], acc)
    ta_core, tb_core = move(ta_near, other_core), move(tb, other_core)
    acc, b_near, ta_core, tb_core = lax.optimization_barrier((acc, b_near, ta_core, tb_core))
    pieces = [ta_core, tb, tb_core, b_near, move(b_near, other_core)]
    frames = samples_here // FINE * XS * ZS * CORES
    return correlate(pieces, acc, 1.0 / frames)[None]


def solution(mesh):
    in_specs = (P("tm", None, "chan", None), P())
    out_specs = P("chan", None, None, "tm")
    return jax.shard_map(shards, mesh=mesh, in_specs=in_specs, out_specs=out_specs, check_vma=False)
```

```python
import functools

import jax
import jax.numpy as jnp
import numpy as np
from jax import lax
from jax.experimental import pallas as pl
from jax.experimental.pallas import tpu as pltpu
from jax.sharding import PartitionSpec as P

FINE = 16
FOUT = 8
TAPS = 16
S = 1024
XS, ZS, CORES = 4, 4, 2
BLOCK = 16
ROWS = 2 * BLOCK
WINDOW = 2 * BLOCK * FINE
VMEM = pltpu.VMEM
F32 = jnp.float32
BF16 = jnp.bfloat16


def place(x, z, c):
    return (x * ZS + z) * CORES + c


def moves(rule):
    out = []
    for x in range(XS):
        for z in range(ZS):
            for c in range(CORES):
                out.append((place(x, z, c), place(*rule(x, z, c))))
    return out


def move(array, rule):
    return lax.ppermute(array, "tm", moves(rule))


def along_x(distance):
    return lambda x, z, c: ((x + distance) % XS, z, c)


def far_z(x, z, c):
    return x, z ^ 2, c


def near_z(x, z, c):
    return x, z ^ 1, c


def other_core(x, z, c):
    return x, z, 1 - c


def halo_of(tail):
    pairs = [(i, i + 1) for i in range(XS * ZS * CORES - 1)]
    return lax.ppermute(tail, "tm", pairs)


def trig_table():
    k = np.arange(FOUT)[:, None]
    n = np.arange(FINE)[None, :]
    phase = (k * n % FINE) * (2.0 * np.pi / FINE)
    c, s = np.cos(phase), np.sin(phase)
    real_row = np.stack([c, s], -1).reshape(FOUT, 2 * FINE)
    imag_row = np.stack([-s, c], -1).reshape(FOUT, 2 * FINE)
    rows = np.stack([real_row, imag_row], 1).reshape(2 * FOUT, 2 * FINE)
    return np.tile(rows.astype(np.float32), (1, 2 * BLOCK))


def spec(n):
    return [pl.BlockSpec(memory_space=VMEM)] * n


def shape(*dims, kind=BF16):
    return jax.ShapeDtypeStruct(dims, kind)


def band_matrix(taps_ref, trig_ref, band_ref):
    me = lax.axis_index("tm")
    x = me // (ZS * CORES)
    odd = me // 4 % 2
    width = 2 * WINDOW
    taps_len = TAPS * FINE
    row = lax.broadcasted_iota(jnp.int32, (taps_len, width), 0)
    col = lax.broadcasted_iota(jnp.int32, (taps_len, width), 1)
    pick = (col // 2 == row).astype(F32)
    taps = jnp.broadcast_to(taps_ref[...], (BLOCK, taps_len))
    twice = lax.dot_general(
        taps, pick, (((1,), (0,)), ((), ())), precision=lax.Precision.HIGHEST, preferred_element_type=F32
    )
    frame = lax.broadcasted_iota(jnp.int32, (BLOCK, width), 0)
    shifted = jnp.zeros((BLOCK, width), F32)
    for f in range(BLOCK):
        shifted = jnp.where(frame == f, pltpu.roll(twice, 2 * FINE * (f + 1) % width, 1), shifted)
    for d in range(XS):
        for other in range(2):
            k = (x + d) % XS * 2 + (odd + other) % 2
            for ro in range(2):
                at = ((d * 2 + other) * 2 + ro) * BLOCK
                wave = trig_ref[pl.ds(k * 2 + ro, 1), :]
                band_ref[at : at + BLOCK, :] = (shifted * wave).astype(BF16)


def tail_copy(volt_ref, out_ref, sem):
    n = out_ref.shape[0]
    copy = pltpu.make_async_copy(volt_ref.at[pl.ds(volt_ref.shape[0] - n, n)], out_ref, sem)
    copy.start()
    copy.wait()


def filter_late(taps_ref, trig_ref, volt_ref, t0, t1, t2, t3, m_ref, band_ref):
    band_matrix(taps_ref, trig_ref, band_ref)
    for i in range(2):
        start = i * BLOCK * FINE
        window = volt_ref[start : start + WINDOW].reshape(2 * WINDOW, S)
        out = jnp.dot(band_ref[...], window, preferred_element_type=F32).astype(BF16)
        rows = slice(i * ROWS, (i + 1) * ROWS)
        for d, t_ref in enumerate((t0, t1, t2, t3)):
            m_ref[d, rows, :] = out[2 * d * ROWS : (2 * d + 1) * ROWS]
            t_ref[rows, :] = out[(2 * d + 1) * ROWS : (2 * d + 2) * ROWS]


def filter_first(halo_ref, volt_ref, band_ref, m_ref, t_ref):
    here = BLOCK * FINE
    own = volt_ref[0:here].reshape(2 * here, S)
    prior = halo_ref[...].reshape(2 * here - 2 * FINE, S)
    band = band_ref[...]
    out = jnp.dot(band[:, 2 * here :], own, preferred_element_type=F32)
    out += jnp.dot(band[:, 2 * FINE : 2 * here], prior, preferred_element_type=F32)
    out = out.astype(BF16)
    for d in range(XS):
        m_ref[d] = out[2 * d * ROWS : (2 * d + 1) * ROWS]
        t_ref[d] = out[(2 * d + 1) * ROWS : (2 * d + 2) * ROWS]


def products(n_pieces, scale, *refs):
    pieces, rest = refs[:n_pieces], refs[n_pieces:]
    out_ref = rest[-1]
    j = pl.program_id(0)
    quarter = lax.axis_index("tm") % 4
    cols = pl.ds(pl.multiple_of(quarter * 256, 256), 256)
    rows = pl.ds(pl.multiple_of(j * 256, 256), 256)
    total = None
    for piece in pieces:
        n = piece.shape[0]
        here = piece[:, cols]
        halves = here.reshape(n // ROWS, 2, BLOCK, 256)
        turned = jnp.stack([halves[:, 1], -halves[:, 0]], 1).reshape(n, 256)
        both = jnp.concatenate([here, turned], 1)
        part = lax.dot_general(
            piece[:, rows], both, (((0,), (0,)), ((), ())), preferred_element_type=F32
        )
        total = part if total is None else total + part
    real, imag = total[:, :256], total[:, 256:]
    if len(rest) > 1:
        real += rest[0][0]
        imag += rest[0][1]
    if scale is not None:
        real, imag = real * scale, imag * scale
    out_ref[0] = real
    out_ref[1] = imag


def correlate(pieces, acc, scale=None, weight=1):
    frames = sum(p.shape[0] for p in pieces)
    block = pl.BlockSpec((2, 256, 256), lambda j: (0, j, 0))
    more = [] if acc is None else [acc]
    return pl.pallas_call(
        functools.partial(products, len(pieces), scale),
        grid=(4,),
        out_shape=shape(2, S, 256, kind=F32),
        in_specs=[pl.BlockSpec(p.shape, lambda j: (0, 0), memory_space=VMEM, pipeline_mode=pl.Buffered(1)) for p in pieces]
        + [block] * len(more),
        out_specs=block,
        compiler_params=pltpu.CompilerParams(vmem_limit_bytes=40 << 20),
        cost_estimate=pl.CostEstimate(flops=2 * weight * frames * S * 512, bytes_accessed=4 << 20, transcendentals=0),
    )(*pieces, *more)


def spread(slabs):
    return [slabs[0]] + [move(slabs[d], along_x(d)) for d in range(1, XS)]


def shards(voltage, taps):
    samples_here = voltage.shape[0]
    volt = voltage.reshape(samples_here, 2, S)
    params = pltpu.CompilerParams(vmem_limit_bytes=40 << 20)
    tail = pl.pallas_call(
        tail_copy,
        out_shape=shape((TAPS - 1) * FINE, 2, S),
        in_specs=[pl.BlockSpec(memory_space=VMEM)],
        out_specs=pl.BlockSpec(memory_space=VMEM),
        scratch_shapes=[pltpu.SemaphoreType.DMA],
        compiler_params=params,
    )(volt)
    halo = halo_of(tail)
    *late_out, band = pl.pallas_call(
        filter_late,
        out_shape=(*[shape(2 * ROWS, S)] * XS, shape(XS, 2 * ROWS, S), shape(16 * BLOCK, 2 * WINDOW)),
        in_specs=spec(3),
        out_specs=spec(XS + 2),
        compiler_params=params,
        cost_estimate=pl.CostEstimate(flops=2 << 29, bytes_accessed=6 << 20, transcendentals=0),
    )(taps.reshape(1, -1), jnp.asarray(trig_table()), volt)
    ma = late_out[XS]
    ma_near = move(ma, near_z)
    ta = spread(late_out[:XS])
    halo, *ta = lax.optimization_barrier((halo, *ta))
    ta = move(jnp.concatenate(ta, 0), far_z)
    first_out = pl.pallas_call(
        filter_first,
        out_shape=[shape(XS, ROWS, S)] * 2,
        in_specs=spec(3),
        out_specs=spec(2),
        compiler_params=params,
        cost_estimate=pl.CostEstimate(flops=1 << 29, bytes_accessed=3 << 20, transcendentals=0),
    )(halo, volt, band)
    mb, tb = first_out
    round_b = spread([jnp.concatenate([tb[d], mb[d], ma[d], ma_near[d]], 0) for d in range(XS)])
    tb = move(jnp.concatenate([slab[:ROWS] for slab in round_b], 0), far_z)
    mb = jnp.concatenate([slab[ROWS : 2 * ROWS] for slab in round_b], 0)
    mine = jnp.concatenate([slab[ROWS:] for slab in round_b], 0)
    ta_near = move(ta, near_z)
    b_near = move(jnp.concatenate([mb, tb], 0), near_z)
    acc = correlate([ta, move(ta, other_core), ta_near], None, weight=64)
    acc = correlate([mine, move(mine, other_core)], acc)
    ta_core = move(ta_near, other_core)
    acc, b_near, ta_core = lax.optimization_barrier((acc, b_near, ta_core))
    last = jnp.concatenate([b_near, tb], 0)
    pieces = [ta_core, last, move(last, other_core)]
    frames = samples_here // FINE * XS * ZS * CORES
    return correlate(pieces, acc, 1.0 / frames)[None]


def solution(mesh):
    in_specs = (P("tm", None, "chan", None), P())
    out_specs = P("chan", None, None, "tm")
    return jax.shard_map(shards, mesh=mesh, in_specs=in_specs, out_specs=out_specs, check_vma=False)
```
